32 devices in a mesh: seq: 8 (over z, y), kv: 4 (over x, core).
Axes of the slice: x: 2, y: 2, z: 4, core: 2. Of those that a mesh axis runs over, the one named last changes fastest.
Arguments:
- queries: bfloat16 [8192, 64, 128], P('seq', 'kv'), may hold values from -256 to 256
- keys: bfloat16 [8192, 8, 128], P('seq', 'kv'), may hold values from -4 to 4
- values: bfloat16 [8192, 8, 128], P('seq', 'kv'), may hold values from -6 to 6
- cluster_ids: int32 [8192], P(('seq', 'kv')), may hold values from 0 to 15, as said below
Outputs:
- attended: bfloat16 [8192, 64, 128], P('seq', 'kv')
The draws below stay inside these ranges and needn't reach their ends.
Inputs may be any that keep to these rules, and one draw needn't show every extreme that they name: `cluster_ids`: every cluster holds exactly 512 tokens. Taking the tokens in aligned blocks of 1024 positions and the clusters in groups o * 2 to (o + 1) * 2 - 1, at most 192 tokens of one block belong to one group, and some block reaches 192 in some group.
All inputs are finite; a program needn't handle non-finite values.
Results may differ from the reference program's by a relative error of at most 0.0046.
Values may be sent and summed in bfloat16 or wider, within the bound.
A program may use at most 128 MiB of HBM per device.

```python
import math
import jax
import jax.numpy as jnp
from jax import lax

QH = 64
KVH = 8
HD = 128
GROUP_SPAN = 512
CLUST_DEV = 2
TOKENS = 8192
N_SEQ = 8


def cluster_draw(key):
    spread_key = jax.random.fold_in(key, 1001)
    transfer_entries = GROUP_SPAN // N_SEQ + max(1, GROUP_SPAN // (2 * N_SEQ))
    others = N_SEQ - 1
    leftover_entries = GROUP_SPAN - transfer_entries
    middle = leftover_entries // others
    leftover = leftover_entries - middle * others
    reach = middle // 2
    ordering = jax.random.permutation(jax.random.fold_in(spread_key, 1), N_SEQ).astype(jnp.int32)
    extra = (jnp.arange(others) < leftover).astype(jnp.int32)
    columns = []
    for part_index in range(CLUST_DEV):
        shake = jax.random.randint(jax.random.fold_in(spread_key, 10 + part_index), (others,), 0, reach + 1).astype(jnp.int32)
        outgoing_counts = middle + extra + shake - jnp.roll(shake, 1)
        device_piece_counts = jnp.concatenate([jnp.full((1,), transfer_entries, jnp.int32), outgoing_counts.astype(jnp.int32)])
        columns.append(jnp.zeros((N_SEQ,), jnp.int32).at[ordering].set(device_piece_counts))
    shares = jnp.stack(columns, axis=1)
    owner_label = jax.random.permutation(jax.random.fold_in(spread_key, 2), N_SEQ).astype(jnp.int32)
    source_label = jax.random.permutation(jax.random.fold_in(spread_key, 3), N_SEQ).astype(jnp.int32)
    offset_table = (owner_label[None, :] - source_label[:, None]) % N_SEQ
    block_counts = shares[offset_table].reshape(N_SEQ, N_SEQ * CLUST_DEV)
    bounds = jnp.cumsum(block_counts, axis=1).astype(jnp.int32)
    positions = jnp.arange(CLUST_DEV * GROUP_SPAN).astype(jnp.int32)
    listed = jnp.sum((bounds[:, None, :] <= positions[None, :, None]).astype(jnp.int32), axis=2).astype(jnp.int32)
    shuffle_keys = jax.random.split(jax.random.fold_in(spread_key, 4), N_SEQ)
    shuffles = jax.vmap(lambda one_key: jax.random.permutation(one_key, CLUST_DEV * GROUP_SPAN))(shuffle_keys).astype(jnp.int32)
    return jnp.take_along_axis(listed, shuffles, axis=1).reshape(N_SEQ * CLUST_DEV * GROUP_SPAN).astype(jnp.int32)


def first_key_position(key):
    raw = jax.random.normal(jax.random.fold_in(key, 77), (TOKENS, KVH, HD), jnp.float32)
    return jnp.clip(raw, -4.0, 4.0)


def draw_cluster_ids(key, part):
    return cluster_draw(key)


def draw_keys(key, part):
    base = first_key_position(key)
    result = base
    return result.astype(jnp.bfloat16)


def draw_queries(key, part):
    key = jax.random.fold_in(key, 5)
    drawn = jnp.clip(jax.random.normal(key, (TOKENS, QH, HD), jnp.float32), -4.0, 4.0)
    return drawn.astype(jnp.bfloat16)


def block_levels(key, shape, cuts, low, high):
    level, own = 1.0, jax.random.fold_in(key, 6)
    for dim, blocks in cuts:
        heights = jnp.exp(jax.random.uniform(jax.random.fold_in(own, dim), (blocks,), jnp.float32, low / len(cuts), high / len(cuts)))
        level = level * jnp.repeat(heights, shape[dim] // blocks).reshape([-1 if axis == dim else 1 for axis in range(len(shape))])
    return level


def scatter_about(own_key, extent, spread, limit, cuts=(), held_as=jnp.bfloat16):
    drawn = spread * jax.random.normal(own_key, extent, jnp.float32)
    if cuts:
        drawn = drawn * block_levels(own_key, extent, cuts, -0.22, 0.18)
    return jnp.clip(drawn, -limit, limit).astype(held_as)


def setup_inputs(seed: int = 0) -> dict:
    key_of = jax.random.split(jax.random.key(seed), 5)
    queries = draw_queries(jax.random.fold_in(key_of[4], 71), 0)
    keys = draw_keys(jax.random.fold_in(key_of[4], 71), 0)
    values = scatter_about(key_of[2], (TOKENS, KVH, HD), 1.0, 6.0, ((0, 8), (1, 4)))
    cluster_ids = draw_cluster_ids(jax.random.fold_in(key_of[4], 71), 0)
    return {"queries": queries, "keys": keys, "values": values, "cluster_ids": cluster_ids}


def reference(queries, keys, values, cluster_ids):
    token_count = cluster_ids.shape[0]
    cluster_count = token_count // GROUP_SPAN
    onehot = (cluster_ids[:, None] == jnp.arange(cluster_count).astype(jnp.int32)[None, :]).astype(jnp.int32)
    before = jnp.cumsum(onehot, axis=0).astype(jnp.int32) - onehot
    cluster_rank = lax.optimization_barrier(jnp.sum(before * onehot, axis=1)).astype(jnp.int32)
    slot_sorted_order = (cluster_ids * GROUP_SPAN + cluster_rank).astype(jnp.int32)
    order = jnp.zeros((token_count,), jnp.int32).at[slot_sorted_order].set(jnp.arange(token_count).astype(jnp.int32))
    group_size = QH // KVH
    q_sorted = queries[order].reshape(cluster_count, GROUP_SPAN, KVH, group_size, HD)
    k_sorted = keys[order].reshape(cluster_count, GROUP_SPAN, KVH, HD)
    v_sorted = values[order].reshape(cluster_count, GROUP_SPAN, KVH, HD)
    causal = jnp.arange(GROUP_SPAN)[:, None] >= jnp.arange(GROUP_SPAN)[None, :]
    score_scale = 1.0 / math.sqrt(HD)

    def attend_cluster(cluster_tile_rows):
        q_block, k_block, v_block = cluster_tile_rows
        scores = jnp.einsum('qkgd,skd->kgqs', q_block.astype(jnp.float32), k_block.astype(jnp.float32)) * score_scale
        scores = jnp.where(causal, scores, -jnp.inf)
        row_max = lax.optimization_barrier(jnp.max(scores, axis=-1, keepdims=True))
        weights = jnp.exp(scores - row_max)
        softmax_weights = (weights / lax.optimization_barrier(jnp.sum(weights, axis=-1, keepdims=True))).astype(jnp.bfloat16)
        mixed = jnp.einsum('kgqs,skd->qkgd', softmax_weights.astype(jnp.float32), v_block.astype(jnp.float32))
        return mixed.astype(jnp.bfloat16)
    out_sorted = lax.map(attend_cluster, (q_sorted, k_sorted, v_sorted))
    return out_sorted.reshape(token_count, QH, HD)[slot_sorted_order]
```

```python
import functools
import math

import jax
import jax.numpy as jnp
from jax import lax
from jax.experimental import pallas as pl
from jax.experimental.pallas import tpu as pltpu
from jax.sharding import PartitionSpec as P

GROUP_SPAN = 512
CLUST_DEV = 2


def prefix(part, axis, combine, identity):
    place = lax.axis_index(axis)
    gathered = lax.all_gather(part, axis)
    state = jnp.zeros_like(part) + jnp.asarray(identity, part.dtype)

    def one(turn, state):
        return combine(state, lax.dynamic_index_in_dim(gathered, turn, 0, False))

    return lax.fori_loop(0, place, one, state)


def source_rows(target_index, slot_total):
    source_total = target_index.shape[0]
    hits = target_index[None, :] == jnp.arange(slot_total, dtype=jnp.int32)[:, None]
    numbers = jnp.arange(source_total, dtype=jnp.int32)[None, :]
    anchor = jnp.sum(jnp.where(hits, numbers, 0), axis=1)
    filled = jnp.any(hits, axis=1)
    return (anchor, filled)


def attend(query_received, k_recv, v_recv, row_slot):
    source_count, slot_count, kv_heads, width = query_received.shape
    head_size = k_recv.shape[3]
    group_size = width // head_size
    tok_rows = CLUST_DEV * GROUP_SPAN
    flat_slot = row_slot.reshape(source_count * slot_count)
    anchor, filled = source_rows(flat_slot, tok_rows)
    q_flat = query_received.reshape(source_count * slot_count, kv_heads, width)
    k_flat = k_recv.reshape(source_count * slot_count, kv_heads, head_size)
    v_flat = v_recv.reshape(source_count * slot_count, kv_heads, head_size)
    live = filled[:, None, None]
    q_rows = jnp.where(live, q_flat[anchor], jnp.zeros((), q_flat.dtype))
    k_rows = jnp.where(live, k_flat[anchor], jnp.zeros((), k_flat.dtype))
    v_rows = jnp.where(live, v_flat[anchor], jnp.zeros((), v_flat.dtype))
    q_rows = q_rows.reshape(CLUST_DEV, GROUP_SPAN, kv_heads, group_size, head_size)
    k_rows = k_rows.reshape(CLUST_DEV, GROUP_SPAN, kv_heads, head_size)
    v_rows = v_rows.reshape(CLUST_DEV, GROUP_SPAN, kv_heads, head_size)
    causal = jnp.arange(GROUP_SPAN)[:, None] >= jnp.arange(GROUP_SPAN)[None, :]
    score_scale = 1.0 / math.sqrt(head_size)
    attention_results = []
    for block_index in range(CLUST_DEV):
        scores = (
            jnp.einsum(
                "qkgd,skd->kgqs",
                q_rows[block_index],
                k_rows[block_index],
                preferred_element_type=jnp.float32,
            )
            * score_scale
        )
        scores = jnp.where(causal, scores, -jnp.inf)
        row_max = jnp.max(scores, axis=-1, keepdims=True)
        weights = jnp.exp(scores - row_max)
        softmax_weights = (weights / jnp.sum(weights, axis=-1, keepdims=True)).astype(jnp.bfloat16)
        mixed = jnp.einsum(
            "kgqs,skd->qkgd",
            softmax_weights,
            v_rows[block_index],
            preferred_element_type=jnp.float32,
        )
        attention_results.append(mixed.astype(jnp.bfloat16).reshape(GROUP_SPAN, kv_heads, width))
    out_sorted = jnp.concatenate(attention_results, axis=0)
    results = out_sorted[jnp.clip(flat_slot, 0, tok_rows - 1)]
    return results.reshape(source_count, slot_count, kv_heads, width)


def shards_by_owner(queries, keys, values, cluster_ids):
    position_numbers = lax.all_gather(cluster_ids, "kv", axis=0, tiled=True)
    tok_rows = position_numbers.shape[0]
    seq_count = lax.axis_size("seq")
    cluster_count = tok_rows // GROUP_SPAN * seq_count
    onehot = (
        position_numbers[:, None] == jnp.arange(cluster_count, dtype=jnp.int32)[None, :]
    ).astype(jnp.int32)
    counts = jnp.sum(onehot, axis=0)
    local_rank = jnp.sum((jnp.cumsum(onehot, axis=0) - onehot) * onehot, axis=1)
    offsets = prefix(
        counts,
        "seq",
        lambda before_part, after_part: before_part + after_part,
        jnp.zeros_like(counts),
    )
    slot_sorted_order = (
        position_numbers * GROUP_SPAN + jnp.sum(onehot * offsets[None, :], axis=1) + local_rank
    ).astype(jnp.int32)
    owner_index = slot_sorted_order // tok_rows
    within = slot_sorted_order % tok_rows
    owner_hot = (owner_index[:, None] == jnp.arange(seq_count, dtype=jnp.int32)[None, :]).astype(
        jnp.int32
    )
    buffer_row = jnp.sum((jnp.cumsum(owner_hot, axis=0) - owner_hot) * owner_hot, axis=1)
    capacity = CLUST_DEV * (GROUP_SPAN // seq_count + max(1, GROUP_SPAN // (2 * seq_count)))
    send_index = owner_index * capacity + buffer_row
    kv_heads = keys.shape[1]
    head_size = keys.shape[2]
    width = queries.shape[1] // kv_heads * head_size
    anchor, filled = source_rows(send_index, seq_count * capacity)
    live = filled[:, None, None]
    q_send = jnp.where(
        live, queries.reshape(tok_rows, kv_heads, width)[anchor], jnp.zeros((), queries.dtype)
    ).reshape(seq_count, capacity, kv_heads, width)
    k_send = jnp.where(live, keys[anchor], jnp.zeros((), keys.dtype)).reshape(
        seq_count, capacity, kv_heads, head_size
    )
    v_send = jnp.where(live, values[anchor], jnp.zeros((), values.dtype)).reshape(
        seq_count, capacity, kv_heads, head_size
    )
    slot_send = jnp.where(filled, within[anchor], -1).reshape(seq_count, capacity)
    query_received, k_recv, v_recv, slot_recv = (
        lax.all_to_all(q_send, "seq", split_axis=0, concat_axis=0, tiled=True),
        lax.all_to_all(k_send, "seq", split_axis=0, concat_axis=0, tiled=True),
        lax.all_to_all(v_send, "seq", split_axis=0, concat_axis=0, tiled=True),
        lax.all_to_all(slot_send, "seq", split_axis=0, concat_axis=0, tiled=True),
    )
    results = attend(query_received, k_recv, v_recv, slot_recv)
    returned = lax.all_to_all(results, "seq", split_axis=0, concat_axis=0, tiled=True)
    mixed = returned.reshape(seq_count * capacity, kv_heads, width)[send_index]
    return mixed.reshape(tok_rows, queries.shape[1], head_size)


CHUNK = 16
TILE = 32
FAR = -1e30
MESH = pl.DeviceIdType.MESH


def ids_kernel(n_seq, n_kv, ids_ref, out_ref, send_sem, recv_sem, own_sem):
    s = lax.axis_index("seq")
    k = lax.axis_index("kv")
    total = n_seq * n_kv
    me = s * n_kv + k
    barrier = pltpu.get_barrier_semaphore()

    def other(i):
        o = lax.rem(me + i, total)
        return {"seq": o // n_kv, "kv": lax.rem(o, n_kv)}

    @pl.loop(1, total)
    def _(i):
        pl.semaphore_signal(barrier, inc=1, device_id=other(i), device_id_type=MESH)

    own = pltpu.make_async_copy(ids_ref, out_ref.at[me], own_sem)
    own.start()
    pl.semaphore_wait(barrier, total - 1)

    def copy(i):
        return pltpu.make_async_remote_copy(
            src_ref=ids_ref,
            dst_ref=out_ref.at[me],
            send_sem=send_sem.at[i],
            recv_sem=recv_sem.at[i],
            device_id=other(i),
            device_id_type=MESH,
        )

    @pl.loop(1, total)
    def _(i):
        copy(i).start()

    @pl.loop(1, total)
    def _(i):
        copy(i).wait()

    own.wait()


def gather_ids(cluster_ids):
    n_seq, n_kv = lax.axis_size("seq"), lax.axis_size("kv")
    total = n_seq * n_kv
    rows = cluster_ids.shape[0] // 128
    return pl.pallas_call(
        functools.partial(ids_kernel, n_seq, n_kv),
        out_shape=jax.ShapeDtypeStruct((total, rows, 128), jnp.int32),
        in_specs=[pl.BlockSpec(memory_space=pltpu.VMEM)],
        out_specs=pl.BlockSpec(memory_space=pltpu.VMEM),
        scratch_shapes=[
            pltpu.SemaphoreType.DMA((total,)),
            pltpu.SemaphoreType.DMA((total,)),
            pltpu.SemaphoreType.DMA,
        ],
        compiler_params=pltpu.CompilerParams(collective_id=0, has_side_effects=True),
        name="gather_ids",
    )(cluster_ids.reshape(rows, 128))


def place(n_z):
    s = lax.axis_index("seq")
    return s // 2, lax.rem(s, 2)


def rows_kernel(n_z, heads, kv_ref, out_ref, send_sem, recv_sem, own_sem):
    z, y = place(n_z)
    me = z * 2 + y
    side = z * 2 + 1 - y
    chunks = kv_ref.shape[2]
    barrier = pltpu.get_barrier_semaphore()

    def greet(cond, device):
        @pl.when(cond)
        def _():
            pl.semaphore_signal(barrier, inc=1, device_id={"seq": device}, device_id_type=MESH)

    greet(z >= 0, side)
    greet(z > 0, me - 2)
    greet(z < n_z - 1, me + 2)

    def slot(h, source):
        return out_ref.at[h, :, pl.ds(source * chunks, chunks)]

    own = pltpu.make_async_copy(
        kv_ref, out_ref.at[:, :, pl.ds(me * chunks, chunks)], own_sem
    )
    own.start()

    def hop(h, source, src, way):
        return pltpu.make_async_remote_copy(
            src_ref=src,
            dst_ref=slot(h, source),
            send_sem=send_sem.at[h, source, way],
            recv_sem=recv_sem.at[h, source],
            device_id={"seq": me + 2 if way == 0 else side},
            device_id_type=MESH,
        )

    peers = 1 + (z > 0).astype(jnp.int32) + (z < n_z - 1).astype(jnp.int32)
    pl.semaphore_wait(barrier, peers)

    for h in range(heads):

        @pl.when(z < n_z - 1)
        def _():
            hop(h, me, kv_ref.at[h], 0).start()

        @pl.when(y == 0)
        def _():
            hop(h, me, kv_ref.at[h], 1).start()

        for back in range(1, n_z):

            @pl.when(z >= back)
            def _():
                source = me - 2 * back
                hop(h, source, slot(h, source), 0).wait_recv()

                @pl.when(z < n_z - 1)
                def _():
                    hop(h, source, slot(h, source), 0).start()

                hop(h, source, slot(h, source), 1).start()

    for h in range(heads):

        @pl.when(y == 1)
        def _():
            hop(h, me - 1, slot(h, me - 1), 1).wait_recv()

        @pl.when(z < n_z - 1)
        def _():
            hop(h, me, kv_ref.at[h], 0).wait_send()

        @pl.when(y == 0)
        def _():
            hop(h, me, kv_ref.at[h], 1).wait_send()

        for back in range(1, n_z):

            @pl.when(z >= back)
            def _():
                source = me - 2 * back
                across = side - 2 * back
                hop(h, across, slot(h, across), 1).wait_recv()

                @pl.when(z < n_z - 1)
                def _():
                    hop(h, source, slot(h, source), 0).wait_send()

                hop(h, source, slot(h, source), 1).wait_send()

    own.wait()


def gather_rows(kv_own):
    n_seq = lax.axis_size("seq")
    heads, two, chunks, chunk, width = kv_own.shape
    return pl.pallas_call(
        functools.partial(rows_kernel, n_seq // 2, heads),
        out_shape=jax.ShapeDtypeStruct((heads, two, n_seq * chunks, chunk, width), kv_own.dtype),
        in_specs=[pl.BlockSpec(memory_space=pl.ANY)],
        out_specs=pl.BlockSpec(memory_space=pl.ANY),
        scratch_shapes=[
            pltpu.SemaphoreType.DMA((heads, n_seq, 2)),
            pltpu.SemaphoreType.DMA((heads, n_seq)),
            pltpu.SemaphoreType.DMA,
        ],
        compiler_params=pltpu.CompilerParams(collective_id=1, has_side_effects=True),
        name="gather_rows",
    )(kv_own)


def attend_kernel(
    tiles, chunk_count, cluster_t, list_t, perm_t, flat_t, info_t,
    q_ref, kv_ref, aug_ref, out_ref, qa, kb, vb, ab, obuf,
):
    tok_rows, q_heads, width = q_ref.shape
    heads = kv_ref.shape[0]
    group = q_heads // heads
    rows = TILE * group
    near = 256
    factor = math.log2(math.e) / math.sqrt(width)
    col = lax.broadcasted_iota(jnp.int32, (rows, near), 1)
    token_row = lax.broadcasted_iota(jnp.int32, (rows, near), 0) // group
    lane = lax.broadcasted_iota(jnp.int32, (rows, 128), 1)

    def one(j, carry):
        c = cluster_t[j]
        base = info_t[0, j]
        rank0 = info_t[1, j]
        shift = info_t[2, j]
        own_cols = info_t[3, j]
        for i in range(TILE):
            token = perm_t[jnp.minimum(base + i, tok_rows - 1)]
            q = q_ref[token].astype(jnp.float32)
            for h in range(heads):
                qa[h, i * group : (i + 1) * group, :] = q[h * group : (h + 1) * group]
        for i in range(chunk_count):
            index = list_t[c * chunk_count + i]
            at = slice(i * CHUNK, (i + 1) * CHUNK)
            ab[at, :] = aug_ref[index]
            for h in range(heads):
                kb[h, at, :] = kv_ref[h, 0, index]
                vb[h, at, :] = kv_ref[h, 1, index]
        mark = jnp.where(lane == c, 1.0, 0.0).astype(jnp.bfloat16)
        hidden = (col - token_row > rank0 - shift) & (col < own_cols)
        for h in range(heads):
            lhs = jnp.concatenate([qa[h].astype(jnp.bfloat16), mark], axis=1)
            rhs = jnp.concatenate([kb[h], ab[...]], axis=1)
            s = lax.dot_general(
                lhs, rhs, (((1,), (1,)), ((), ())), preferred_element_type=jnp.float32
            )
            s = jnp.concatenate([jnp.where(hidden, FAR, s[:, :near]), s[:, near:]], axis=1)
            top = jnp.max(s, axis=1, keepdims=True)
            w = jnp.exp2((s - top) * factor)
            w = w * (1.0 / jnp.sum(w, axis=1, keepdims=True))
            o = jnp.dot(w.astype(jnp.bfloat16), vb[h], preferred_element_type=jnp.float32)
            obuf[h, pl.ds(j * TILE, TILE)] = o.reshape(TILE, group, width)
        return carry

    lax.fori_loop(0, tiles, one, 0)

    def put(i, carry):
        for k in range(8):
            t = i * 8 + k
            row = flat_t[t]
            both = jnp.concatenate([obuf[h, row] for h in range(heads)], axis=0)
            out_ref[t] = both.astype(out_ref.dtype)
        return carry

    lax.fori_loop(0, tok_rows // 8, put, 0)


def plan(ids, n_seq):
    i32, bf16, f32 = jnp.int32, jnp.bfloat16, jnp.float32
    tok_rows = ids.shape[1]
    clusters = n_seq * tok_rows // GROUP_SPAN
    chunks = tok_rows // CHUNK
    me = lax.axis_index("seq")
    numbers = jnp.arange(clusters, dtype=i32)
    counts = jnp.sum((ids[:, None, :] == numbers[None, :, None]).astype(i32), axis=2)
    before = (numbers[:, None] < numbers[None, :]).astype(i32)
    start = jnp.sum(counts[:, :, None] * before[None], axis=1)

    ids_me = lax.dynamic_index_in_dim(ids, me, 0, False)
    n_me = lax.dynamic_index_in_dim(counts, me, 0, False)
    start_me = lax.dynamic_index_in_dim(start, me, 0, False)
    where_t = jnp.arange(tok_rows, dtype=i32)
    earlier = (where_t[None, :] < where_t[:, None]) & (ids_me[None, :] == ids_me[:, None])
    rank = jnp.sum(earlier.astype(i32), axis=1)
    hot = (ids_me[:, None] == numbers[None, :]).astype(i32)
    slot = jnp.sum(hot * start_me[None, :], axis=1) + rank
    take = slot[None, :] == where_t[:, None]
    perm = jnp.sum(jnp.where(take, where_t[None, :], 0), axis=1)

    tile_n = (n_me + TILE - 1) // TILE
    tile_start = jnp.sum(tile_n[:, None] * before, axis=0)
    flat = jnp.sum(hot * tile_start[None, :], axis=1) * TILE + rank
    tiles = tok_rows // TILE + clusters
    turn = jnp.arange(tiles, dtype=i32)
    cluster = jnp.sum((tile_start[None, :] + tile_n[None, :] <= turn[:, None]).astype(i32), axis=1)
    cluster = jnp.minimum(cluster, clusters - 1)
    tile_hot = (cluster[:, None] == numbers[None, :]).astype(i32)
    pick = lambda v: jnp.sum(tile_hot * v[None, :], axis=1)
    rank0 = (turn - pick(tile_start)) * TILE
    base = pick(start_me) + rank0

    low = start // CHUNK
    high = (start + counts + CHUNK - 1) // CHUNK
    seen = (jnp.arange(n_seq, dtype=i32) <= me)[:, None] & (counts > 0)
    span = jnp.where(seen, high - low, 0)
    sources = jnp.arange(n_seq, dtype=i32)
    later = (sources[:, None] > sources[None, :]).astype(i32)
    ahead = jnp.sum(span[:, None, :] * later[:, :, None], axis=0)
    chunk_count = (GROUP_SPAN + (2 * CHUNK - 2) * n_seq) // CHUNK
    chunk_count = (chunk_count + 7) // 8 * 8
    at = jnp.arange(chunk_count, dtype=i32)[None, :, None]
    off = at - ahead.T[:, None, :]
    inside = (off >= 0) & (off < span.T[:, None, :])
    index = sources[None, None, :] * chunks + low.T[:, None, :] + off
    none = me * chunks + jnp.where(start_me >= CHUNK, 0, chunks - 1)
    listed = jnp.sum(jnp.where(inside, index, 0), axis=2)
    listed = jnp.where(jnp.any(inside, axis=2), listed, none[:, None])

    low_me = lax.dynamic_index_in_dim(low, me, 0, False)
    span_me = lax.dynamic_index_in_dim(span, me, 0, False)
    info = jnp.stack([base, rank0, pick(low_me * CHUNK - start_me), pick(span_me) * CHUNK])

    lane = jnp.arange(128, dtype=i32)
    pad = lambda v: jnp.pad(v, ((0, 0), (0, 128 - clusters)))
    r = where_t[None, :, None]
    within = (r >= pad(start)[:, None, :]) & (r < pad(start + counts)[:, None, :])
    aug = jnp.where(within, 0.0, FAR).astype(bf16)
    aug = aug.reshape(n_seq * chunks, CHUNK, 128)
    return take, (cluster, listed.reshape(-1), perm, flat, info), aug, tiles, chunk_count


def shards_by_rows(queries, keys, values, cluster_ids):
    n_seq = lax.axis_size("seq")
    tok_rows, heads, width = keys.shape
    chunks = tok_rows // CHUNK
    ids = gather_ids(cluster_ids).reshape(n_seq, tok_rows)
    take, tables, aug, tiles, chunk_count = plan(ids, n_seq)
    pair = jnp.concatenate([keys, values], axis=1).reshape(tok_rows, 2 * heads * width)
    moved = jnp.dot(take.astype(jnp.bfloat16), pair, preferred_element_type=jnp.float32)
    moved = moved.astype(jnp.bfloat16).reshape(chunks, CHUNK, 2, heads, width)
    kv_own = jnp.transpose(moved, (3, 2, 0, 1, 4))
    kv = gather_rows(kv_own)
    group = queries.shape[1] // heads
    rows = TILE * group
    span = chunk_count * CHUNK
    vmem = pl.BlockSpec(memory_space=pltpu.VMEM)
    smem = pl.BlockSpec(memory_space=pltpu.SMEM)
    return pl.pallas_call(
        functools.partial(attend_kernel, tiles, chunk_count),
        out_shape=jax.ShapeDtypeStruct(queries.shape, queries.dtype),
        in_specs=[smem] * 5 + [vmem] * 3,
        out_specs=vmem,
        scratch_shapes=[
            pltpu.VMEM((heads, rows, width), jnp.float32),
            pltpu.VMEM((heads, span, width), jnp.bfloat16),
            pltpu.VMEM((heads, span, width), jnp.bfloat16),
            pltpu.VMEM((span, 128), jnp.bfloat16),
            pltpu.VMEM((heads, tiles * TILE, group, width), jnp.float32),
        ],
        compiler_params=pltpu.CompilerParams(vmem_limit_bytes=56 * 2**20),
        name="attend_rows",
    )(*tables, queries, kv, aug)


def solution(mesh):
    in_specs = (P("seq", "kv", None), P("seq", "kv", None), P("seq", "kv", None), P(("seq", "kv")))
    out_specs = P("seq", "kv", None)
    fits = mesh.shape["seq"] <= 8 and mesh.shape["seq"] % 2 == 0
    body = shards_by_rows if fits else shards_by_owner
    return jax.shard_map(body, mesh=mesh, in_specs=in_specs, out_specs=out_specs, check_vma=False)
```

```python
import functools
import math

import jax
import jax.numpy as jnp
from jax import lax
from jax.experimental import pallas as pl
from jax.experimental.pallas import tpu as pltpu
from jax.sharding import PartitionSpec as P

GROUP_SPAN = 512
CLUST_DEV = 2


def prefix(part, axis, combine, identity):
    place = lax.axis_index(axis)
    gathered = lax.all_gather(part, axis)
    state = jnp.zeros_like(part) + jnp.asarray(identity, part.dtype)

    def one(turn, state):
        return combine(state, lax.dynamic_index_in_dim(gathered, turn, 0, False))

    return lax.fori_loop(0, place, one, state)


def source_rows(target_index, slot_total):
    source_total = target_index.shape[0]
    hits = target_index[None, :] == jnp.arange(slot_total, dtype=jnp.int32)[:, None]
    numbers = jnp.arange(source_total, dtype=jnp.int32)[None, :]
    anchor = jnp.sum(jnp.where(hits, numbers, 0), axis=1)
    filled = jnp.any(hits, axis=1)
    return (anchor, filled)


def attend(query_received, k_recv, v_recv, row_slot):
    source_count, slot_count, kv_heads, width = query_received.shape
    head_size = k_recv.shape[3]
    group_size = width // head_size
    tok_rows = CLUST_DEV * GROUP_SPAN
    flat_slot = row_slot.reshape(source_count * slot_count)
    anchor, filled = source_rows(flat_slot, tok_rows)
    q_flat = query_received.reshape(source_count * slot_count, kv_heads, width)
    k_flat = k_recv.reshape(source_count * slot_count, kv_heads, head_size)
    v_flat = v_recv.reshape(source_count * slot_count, kv_heads, head_size)
    live = filled[:, None, None]
    q_rows = jnp.where(live, q_flat[anchor], jnp.zeros((), q_flat.dtype))
    k_rows = jnp.where(live, k_flat[anchor], jnp.zeros((), k_flat.dtype))
    v_rows = jnp.where(live, v_flat[anchor], jnp.zeros((), v_flat.dtype))
    q_rows = q_rows.reshape(CLUST_DEV, GROUP_SPAN, kv_heads, group_size, head_size)
    k_rows = k_rows.reshape(CLUST_DEV, GROUP_SPAN, kv_heads, head_size)
    v_rows = v_rows.reshape(CLUST_DEV, GROUP_SPAN, kv_heads, head_size)
    causal = jnp.arange(GROUP_SPAN)[:, None] >= jnp.arange(GROUP_SPAN)[None, :]
    score_scale = 1.0 / math.sqrt(head_size)
    attention_results = []
    for block_index in range(CLUST_DEV):
        scores = (
            jnp.einsum(
                "qkgd,skd->kgqs",
                q_rows[block_index],
                k_rows[block_index],
                preferred_element_type=jnp.float32,
            )
            * score_scale
        )
        scores = jnp.where(causal, scores, -jnp.inf)
        row_max = jnp.max(scores, axis=-1, keepdims=True)
        weights = jnp.exp(scores - row_max)
        softmax_weights = (weights / jnp.sum(weights, axis=-1, keepdims=True)).astype(jnp.bfloat16)
        mixed = jnp.einsum(
            "kgqs,skd->qkgd",
            softmax_weights,
            v_rows[block_index],
            preferred_element_type=jnp.float32,
        )
        attention_results.append(mixed.astype(jnp.bfloat16).reshape(GROUP_SPAN, kv_heads, width))
    out_sorted = jnp.concatenate(attention_results, axis=0)
    results = out_sorted[jnp.clip(flat_slot, 0, tok_rows - 1)]
    return results.reshape(source_count, slot_count, kv_heads, width)


def shards_by_owner(queries, keys, values, cluster_ids):
    position_numbers = lax.all_gather(cluster_ids, "kv", axis=0, tiled=True)
    tok_rows = position_numbers.shape[0]
    seq_count = lax.axis_size("seq")
    cluster_count = tok_rows // GROUP_SPAN * seq_count
    onehot = (
        position_numbers[:, None] == jnp.arange(cluster_count, dtype=jnp.int32)[None, :]
    ).astype(jnp.int32)
    counts = jnp.sum(onehot, axis=0)
    local_rank = jnp.sum((jnp.cumsum(onehot, axis=0) - onehot) * onehot, axis=1)
    offsets = prefix(
        counts,
        "seq",
        lambda before_part, after_part: before_part + after_part,
        jnp.zeros_like(counts),
    )
    slot_sorted_order = (
        position_numbers * GROUP_SPAN + jnp.sum(onehot * offsets[None, :], axis=1) + local_rank
    ).astype(jnp.int32)
    owner_index = slot_sorted_order // tok_rows
    within = slot_sorted_order % tok_rows
    owner_hot = (owner_index[:, None] == jnp.arange(seq_count, dtype=jnp.int32)[None, :]).astype(
        jnp.int32
    )
    buffer_row = jnp.sum((jnp.cumsum(owner_hot, axis=0) - owner_hot) * owner_hot, axis=1)
    capacity = CLUST_DEV * (GROUP_SPAN // seq_count + max(1, GROUP_SPAN // (2 * seq_count)))
    send_index = owner_index * capacity + buffer_row
    kv_heads = keys.shape[1]
    head_size = keys.shape[2]
    width = queries.shape[1] // kv_heads * head_size
    anchor, filled = source_rows(send_index, seq_count * capacity)
    live = filled[:, None, None]
    q_send = jnp.where(
        live, queries.reshape(tok_rows, kv_heads, width)[anchor], jnp.zeros((), queries.dtype)
    ).reshape(seq_count, capacity, kv_heads, width)
    k_send = jnp.where(live, keys[anchor], jnp.zeros((), keys.dtype)).reshape(
        seq_count, capacity, kv_heads, head_size
    )
    v_send = jnp.where(live, values[anchor], jnp.zeros((), values.dtype)).reshape(
        seq_count, capacity, kv_heads, head_size
    )
    slot_send = jnp.where(filled, within[anchor], -1).reshape(seq_count, capacity)
    query_received, k_recv, v_recv, slot_recv = (
        lax.all_to_all(q_send, "seq", split_axis=0, concat_axis=0, tiled=True),
        lax.all_to_all(k_send, "seq", split_axis=0, concat_axis=0, tiled=True),
        lax.all_to_all(v_send, "seq", split_axis=0, concat_axis=0, tiled=True),
        lax.all_to_all(slot_send, "seq", split_axis=0, concat_axis=0, tiled=True),
    )
    results = attend(query_received, k_recv, v_recv, slot_recv)
    returned = lax.all_to_all(results, "seq", split_axis=0, concat_axis=0, tiled=True)
    mixed = returned.reshape(seq_count * capacity, kv_heads, width)[send_index]
    return mixed.reshape(tok_rows, queries.shape[1], head_size)


CHUNK = 16
TILE = 32
FAR = -1e30
MESH = pl.DeviceIdType.MESH


def ids_kernel(n_seq, n_kv, ids_ref, out_ref, send_sem, recv_sem, own_sem):
    s = lax.axis_index("seq")
    k = lax.axis_index("kv")
    total = n_seq * n_kv
    me = s * n_kv + k
    barrier = pltpu.get_barrier_semaphore()

    def other(i):
        o = lax.rem(me + i, total)
        return {"seq": o // n_kv, "kv": lax.rem(o, n_kv)}

    @pl.loop(1, total)
    def _(i):
        pl.semaphore_signal(barrier, inc=1, device_id=other(i), device_id_type=MESH)

    own = pltpu.make_async_copy(ids_ref, out_ref.at[me], own_sem)
    own.start()
    pl.semaphore_wait(barrier, total - 1)

    def copy(i):
        return pltpu.make_async_remote_copy(
            src_ref=ids_ref,
            dst_ref=out_ref.at[me],
            send_sem=send_sem.at[i],
            recv_sem=recv_sem.at[i],
            device_id=other(i),
            device_id_type=MESH,
        )

    @pl.loop(1, total)
    def _(i):
        copy(i).start()

    @pl.loop(1, total)
    def _(i):
        copy(i).wait()

    own.wait()


def gather_ids(cluster_ids):
    n_seq, n_kv = lax.axis_size("seq"), lax.axis_size("kv")
    total = n_seq * n_kv
    rows = cluster_ids.shape[0] // 128
    return pl.pallas_call(
        functools.partial(ids_kernel, n_seq, n_kv),
        out_shape=jax.ShapeDtypeStruct((total, rows, 128), jnp.int32),
        in_specs=[pl.BlockSpec(memory_space=pltpu.VMEM)],
        out_specs=pl.BlockSpec(memory_space=pltpu.VMEM),
        scratch_shapes=[
            pltpu.SemaphoreType.DMA((total,)),
            pltpu.SemaphoreType.DMA((total,)),
            pltpu.SemaphoreType.DMA,
        ],
        compiler_params=pltpu.CompilerParams(collective_id=0, has_side_effects=True),
        name="gather_ids",
    )(cluster_ids.reshape(rows, 128))


def place(n_z):
    s = lax.axis_index("seq")
    return s // 2, lax.rem(s, 2)


def rows_kernel(
    n_z, heads, kv_ref, out_ref, send_sem, recv_sem, extra_send, extra_recv, own_sem
):
    z, y = place(n_z)
    me = z * 2 + y
    side = z * 2 + 1 - y
    chunks = kv_ref.shape[2]
    barrier = pltpu.get_barrier_semaphore()

    def greet(cond, device):
        @pl.when(cond)
        def _():
            pl.semaphore_signal(barrier, inc=1, device_id={"seq": device}, device_id_type=MESH)

    greet(z >= 0, side)
    greet(z > 0, me - 2)
    greet(z < n_z - 1, me + 2)

    def slot(h, source):
        return out_ref.at[h, :, pl.ds(source * chunks, chunks)]

    own = pltpu.make_async_copy(
        kv_ref, out_ref.at[:, :, pl.ds(me * chunks, chunks)], own_sem
    )
    own.start()

    def hop(h, source, src, way):
        return pltpu.make_async_remote_copy(
            src_ref=src,
            dst_ref=slot(h, source),
            send_sem=send_sem.at[h, source, way],
            recv_sem=recv_sem.at[h, source],
            device_id={"seq": me + 2 if way == 0 else side},
            device_id_type=MESH,
        )

    peers = 1 + (z > 0).astype(jnp.int32) + (z < n_z - 1).astype(jnp.int32)
    pl.semaphore_wait(barrier, peers)

    last = z == n_z - 1
    turn = (z == n_z - 2) & (y == 1)

    def half(h, source, part):
        return out_ref.at[h, part, pl.ds(source * chunks, chunks)]

    def first_half(h, source):
        return pltpu.make_async_remote_copy(
            src_ref=half(h, source, 0),
            dst_ref=half(h, source, 0),
            send_sem=send_sem.at[h, source, 1],
            recv_sem=recv_sem.at[h, source],
            device_id={"seq": side},
            device_id_type=MESH,
        )

    def second_half(h, source):
        return pltpu.make_async_remote_copy(
            src_ref=half(h, source, 1),
            dst_ref=half(h, source, 1),
            send_sem=extra_send.at[h],
            recv_sem=extra_recv.at[h],
            device_id={"seq": me + 2},
            device_id_type=MESH,
        )

    for h in range(heads):

        @pl.when(z < n_z - 1)
        def _():
            hop(h, me, kv_ref.at[h], 0).start()

        @pl.when(y == 0)
        def _():
            hop(h, me, kv_ref.at[h], 1).start()

        for back in range(1, n_z):

            @pl.when(z >= back)
            def _():
                source = me - 2 * back
                hop(h, source, slot(h, source), 0).wait_recv()

                @pl.when(z < n_z - 1)
                def _():
                    hop(h, source, slot(h, source), 0).start()

                if back > 1:
                    hop(h, source, slot(h, source), 1).start()
                else:

                    @pl.when(last & (y == 0))
                    def _():
                        first_half(h, source).start()

                    @pl.when(jnp.logical_not(last & (y == 0)))
                    def _():
                        hop(h, source, slot(h, source), 1).start()

        @pl.when(turn)
        def _():
            hop(h, me - 1, slot(h, me - 1), 1).wait_recv()
            second_half(h, me - 1).start()

    for h in range(heads):

        @pl.when((y == 1) & jnp.logical_not(turn))
        def _():
            hop(h, me - 1, slot(h, me - 1), 1).wait_recv()

        @pl.when(turn)
        def _():
            second_half(h, me - 1).wait_send()

        @pl.when(z < n_z - 1)
        def _():
            hop(h, me, kv_ref.at[h], 0).wait_send()

        @pl.when(y == 0)
        def _():
            hop(h, me, kv_ref.at[h], 1).wait_send()

        for back in range(1, n_z):

            @pl.when(z >= back)
            def _():
                source = me - 2 * back
                across = side - 2 * back

                @pl.when(z < n_z - 1)
                def _():
                    hop(h, source, slot(h, source), 0).wait_send()

                if back > 1:
                    hop(h, across, slot(h, across), 1).wait_recv()
                    hop(h, source, slot(h, source), 1).wait_send()
                else:

                    @pl.when(last & (y == 0))
                    def _():
                        first_half(h, source).wait_send()

                    @pl.when(jnp.logical_not(last & (y == 0)))
                    def _():
                        hop(h, source, slot(h, source), 1).wait_send()

                    @pl.when(last & (y == 1))
                    def _():
                        first_half(h, across).wait_recv()
                        second_half(h, across).wait_recv()

                    @pl.when(jnp.logical_not(last & (y == 1)))
                    def _():
                        hop(h, across, slot(h, across), 1).wait_recv()

    own.wait()


def gather_rows(kv_own):
    n_seq = lax.axis_size("seq")
    heads, two, chunks, chunk, width = kv_own.shape
    return pl.pallas_call(
        functools.partial(rows_kernel, n_seq // 2, heads),
        out_shape=jax.ShapeDtypeStruct((heads, two, n_seq * chunks, chunk, width), kv_own.dtype),
        in_specs=[pl.BlockSpec(memory_space=pl.ANY)],
        out_specs=pl.BlockSpec(memory_space=pl.ANY),
        scratch_shapes=[
            pltpu.SemaphoreType.DMA((heads, n_seq, 2)),
            pltpu.SemaphoreType.DMA((heads, n_seq)),
            pltpu.SemaphoreType.DMA((heads,)),
            pltpu.SemaphoreType.DMA((heads,)),
            pltpu.SemaphoreType.DMA,
        ],
        compiler_params=pltpu.CompilerParams(collective_id=1, has_side_effects=True),
        name="gather_rows",
    )(kv_own)


def attend_kernel(
    tiles, chunk_count, cluster_t, list_t, perm_t, flat_t, info_t,
    q_ref, kv_ref, aug_ref, out_ref, qa, kb, vb, ab, obuf,
):
    tok_rows, q_heads, width = q_ref.shape
    heads = kv_ref.shape[0]
    group = q_heads // heads
    rows = TILE * group
    near = 256
    factor = math.log2(math.e) / math.sqrt(width)
    col = lax.broadcasted_iota(jnp.int32, (rows, near), 1)
    token_row = lax.broadcasted_iota(jnp.int32, (rows, near), 0) // group
    lane = lax.broadcasted_iota(jnp.int32, (rows, 128), 1)

    def one(j, carry):
        c = cluster_t[j]
        base = info_t[0, j]
        rank0 = info_t[1, j]
        shift = info_t[2, j]
        own_cols = info_t[3, j]
        for i in range(TILE):
            token = perm_t[jnp.minimum(base + i, tok_rows - 1)]
            q = q_ref[token].astype(jnp.float32)
            for h in range(heads):
                qa[h, i * group : (i + 1) * group, :] = q[h * group : (h + 1) * group]
        for i in range(chunk_count):
            index = list_t[c * chunk_count + i]
            at = slice(i * CHUNK, (i + 1) * CHUNK)
            ab[at, :] = aug_ref[index]
            for h in range(heads):
                kb[h, at, :] = kv_ref[h, 0, index]
                vb[h, at, :width] = kv_ref[h, 1, index]
        mark = jnp.where(lane == c, 1.0, 0.0).astype(jnp.bfloat16)
        hidden = (col - token_row > rank0 - shift) & (col < own_cols)
        for h in range(heads):
            lhs = jnp.concatenate([qa[h].astype(jnp.bfloat16), mark], axis=1)
            rhs = jnp.concatenate([kb[h], ab[...]], axis=1)
            s = lax.dot_general(
                lhs, rhs, (((1,), (1,)), ((), ())), preferred_element_type=jnp.float32
            )
            s = jnp.concatenate([jnp.where(hidden, FAR, s[:, :near]), s[:, near:]], axis=1)
            top = jnp.max(s, axis=1, keepdims=True)
            w = jnp.exp2((s - top) * factor)
            o = jnp.dot(w.astype(jnp.bfloat16), vb[h], preferred_element_type=jnp.float32)
            o = o[:, :width] / o[:, width:]
            obuf[h, pl.ds(j * TILE, TILE)] = o.reshape(TILE, group, width)
        return carry

    vb[:, :, width:] = jnp.ones((heads, vb.shape[1], width), jnp.bfloat16)
    lax.fori_loop(0, info_t[4, 0], one, 0)

    def put(i, carry):
        for k in range(8):
            t = i * 8 + k
            row = flat_t[t]
            both = jnp.concatenate([obuf[h, row] for h in range(heads)], axis=0)
            out_ref[t] = both.astype(out_ref.dtype)
        return carry

    lax.fori_loop(0, tok_rows // 8, put, 0)


def plan(ids, n_seq):
    i32, bf16, f32 = jnp.int32, jnp.bfloat16, jnp.float32
    tok_rows = ids.shape[1]
    clusters = n_seq * tok_rows // GROUP_SPAN
    chunks = tok_rows // CHUNK
    me = lax.axis_index("seq")
    numbers = jnp.arange(clusters, dtype=i32)
    counts = jnp.sum((ids[:, None, :] == numbers[None, :, None]).astype(i32), axis=2)
    before = (numbers[:, None] < numbers[None, :]).astype(i32)
    start = jnp.sum(counts[:, :, None] * before[None], axis=1)

    ids_me = lax.dynamic_index_in_dim(ids, me, 0, False)
    n_me = lax.dynamic_index_in_dim(counts, me, 0, False)
    start_me = lax.dynamic_index_in_dim(start, me, 0, False)
    where_t = jnp.arange(tok_rows, dtype=i32)
    earlier = (where_t[None, :] < where_t[:, None]) & (ids_me[None, :] == ids_me[:, None])
    rank = jnp.sum(earlier.astype(i32), axis=1)
    hot = (ids_me[:, None] == numbers[None, :]).astype(i32)
    slot = jnp.sum(hot * start_me[None, :], axis=1) + rank
    take = slot[None, :] == where_t[:, None]
    perm = jnp.sum(jnp.where(take, where_t[None, :], 0), axis=1)

    tile_n = (n_me + TILE - 1) // TILE
    tile_start = jnp.sum(tile_n[:, None] * before, axis=0)
    flat = jnp.sum(hot * tile_start[None, :], axis=1) * TILE + rank
    tiles = tok_rows // TILE + clusters
    turn = jnp.arange(tiles, dtype=i32)
    cluster = jnp.sum((tile_start[None, :] + tile_n[None, :] <= turn[:, None]).astype(i32), axis=1)
    cluster = jnp.minimum(cluster, clusters - 1)
    tile_hot = (cluster[:, None] == numbers[None, :]).astype(i32)
    pick = lambda v: jnp.sum(tile_hot * v[None, :], axis=1)
    rank0 = (turn - pick(tile_start)) * TILE
    base = pick(start_me) + rank0

    low = start // CHUNK
    high = (start + counts + CHUNK - 1) // CHUNK
    seen = (jnp.arange(n_seq, dtype=i32) <= me)[:, None] & (counts > 0)
    span = jnp.where(seen, high - low, 0)
    sources = jnp.arange(n_seq, dtype=i32)
    later = (sources[:, None] > sources[None, :]).astype(i32)
    ahead = jnp.sum(span[:, None, :] * later[:, :, None], axis=0)
    chunk_count = (GROUP_SPAN + (2 * CHUNK - 2) * n_seq) // CHUNK
    chunk_count = (chunk_count + 7) // 8 * 8
    at = jnp.arange(chunk_count, dtype=i32)[None, :, None]
    off = at - ahead.T[:, None, :]
    inside = (off >= 0) & (off < span.T[:, None, :])
    index = sources[None, None, :] * chunks + low.T[:, None, :] + off
    none = me * chunks + jnp.where(start_me >= CHUNK, 0, chunks - 1)
    listed = jnp.sum(jnp.where(inside, index, 0), axis=2)
    listed = jnp.where(jnp.any(inside, axis=2), listed, none[:, None])

    low_me = lax.dynamic_index_in_dim(low, me, 0, False)
    span_me = lax.dynamic_index_in_dim(span, me, 0, False)
    info = jnp.stack([base, rank0, pick(low_me * CHUNK - start_me), pick(span_me) * CHUNK, jnp.full_like(base, jnp.sum(tile_n))])

    lane = jnp.arange(128, dtype=i32)
    pad = lambda v: jnp.pad(v, ((0, 0), (0, 128 - clusters)))
    r = where_t[None, :, None]
    within = (r >= pad(start)[:, None, :]) & (r < pad(start + counts)[:, None, :])
    aug = jnp.where(within, 0.0, FAR).astype(bf16)
    aug = aug.reshape(n_seq * chunks, CHUNK, 128)
    return take, (cluster, listed.reshape(-1), perm, flat, info), aug, tiles, chunk_count


def shards_by_rows(queries, keys, values, cluster_ids):
    n_seq = lax.axis_size("seq")
    tok_rows, heads, width = keys.shape
    chunks = tok_rows // CHUNK
    ids = gather_ids(cluster_ids).reshape(n_seq, tok_rows)
    take, tables, aug, tiles, chunk_count = plan(ids, n_seq)
    pair = jnp.concatenate([keys, values], axis=1).reshape(tok_rows, 2 * heads * width)
    moved = jnp.dot(take.astype(jnp.bfloat16), pair, preferred_element_type=jnp.float32)
    moved = moved.astype(jnp.bfloat16).reshape(chunks, CHUNK, 2, heads, width)
    kv_own = jnp.transpose(moved, (3, 2, 0, 1, 4))
    kv = gather_rows(kv_own)
    group = queries.shape[1] // heads
    rows = TILE * group
    span = chunk_count * CHUNK
    vmem = pl.BlockSpec(memory_space=pltpu.VMEM)
    smem = pl.BlockSpec(memory_space=pltpu.SMEM)
    return pl.pallas_call(
        functools.partial(attend_kernel, tiles, chunk_count),
        out_shape=jax.ShapeDtypeStruct(queries.shape, queries.dtype),
        in_specs=[smem] * 5 + [vmem] * 3,
        out_specs=vmem,
        scratch_shapes=[
            pltpu.VMEM((heads, rows, width), jnp.float32),
            pltpu.VMEM((heads, span, width), jnp.bfloat16),
            pltpu.VMEM((heads, span, 2 * width), jnp.bfloat16),
            pltpu.VMEM((span, 128), jnp.bfloat16),
            pltpu.VMEM((heads, tiles * TILE, group, width), jnp.float32),
        ],
        compiler_params=pltpu.CompilerParams(vmem_limit_bytes=56 * 2**20),
        name="attend_rows",
    )(*tables, queries, kv, aug)


def solution(mesh):
    in_specs = (P("seq", "kv", None), P("seq", "kv", None), P("seq", "kv", None), P(("seq", "kv")))
    out_specs = P("seq", "kv", None)
    fits = 4 <= mesh.shape["seq"] <= 8 and mesh.shape["seq"] % 2 == 0
    body = shards_by_rows if fits else shards_by_owner
    return jax.shard_map(body, mesh=mesh, in_specs=in_specs, out_specs=out_specs, check_vma=False)
```

```python
import functools
import math

import jax
import jax.numpy as jnp
from jax import lax
from jax.experimental import pallas as pl
from jax.experimental.pallas import tpu as pltpu
from jax.sharding import PartitionSpec as P

GROUP_SPAN = 512
CLUST_DEV = 2


def prefix(part, axis, combine, identity):
    place = lax.axis_index(axis)
    gathered = lax.all_gather(part, axis)
    state = jnp.zeros_like(part) + jnp.asarray(identity, part.dtype)

    def one(turn, state):
        return combine(state, lax.dynamic_index_in_dim(gathered, turn, 0, False))

    return lax.fori_loop(0, place, one, state)


def source_rows(target_index, slot_total):
    source_total = target_index.shape[0]
    hits = target_index[None, :] == jnp.arange(slot_total, dtype=jnp.int32)[:, None]
    numbers = jnp.arange(source_total, dtype=jnp.int32)[None, :]
    anchor = jnp.sum(jnp.where(hits, numbers, 0), axis=1)
    filled = jnp.any(hits, axis=1)
    return (anchor, filled)


def attend(query_received, k_recv, v_recv, row_slot):
    source_count, slot_count, kv_heads, width = query_received.shape
    head_size = k_recv.shape[3]
    group_size = width // head_size
    tok_rows = CLUST_DEV * GROUP_SPAN
    flat_slot = row_slot.reshape(source_count * slot_count)
    anchor, filled = source_rows(flat_slot, tok_rows)
    q_flat = query_received.reshape(source_count * slot_count, kv_heads, width)
    k_flat = k_recv.reshape(source_count * slot_count, kv_heads, head_size)
    v_flat = v_recv.reshape(source_count * slot_count, kv_heads, head_size)
    live = filled[:, None, None]
    q_rows = jnp.where(live, q_flat[anchor], jnp.zeros((), q_flat.dtype))
    k_rows = jnp.where(live, k_flat[anchor], jnp.zeros((), k_flat.dtype))
    v_rows = jnp.where(live, v_flat[anchor], jnp.zeros((), v_flat.dtype))
    q_rows = q_rows.reshape(CLUST_DEV, GROUP_SPAN, kv_heads, group_size, head_size)
    k_rows = k_rows.reshape(CLUST_DEV, GROUP_SPAN, kv_heads, head_size)
    v_rows = v_rows.reshape(CLUST_DEV, GROUP_SPAN, kv_heads, head_size)
    causal = jnp.arange(GROUP_SPAN)[:, None] >= jnp.arange(GROUP_SPAN)[None, :]
    score_scale = 1.0 / math.sqrt(head_size)
    attention_results = []
    for block_index in range(CLUST_DEV):
        scores = (
            jnp.einsum(
                "qkgd,skd->kgqs",
                q_rows[block_index],
                k_rows[block_index],
                preferred_element_type=jnp.float32,
            )
            * score_scale
        )
        scores = jnp.where(causal, scores, -jnp.inf)
        row_max = jnp.max(scores, axis=-1, keepdims=True)
        weights = jnp.exp(scores - row_max)
        softmax_weights = (weights / jnp.sum(weights, axis=-1, keepdims=True)).astype(jnp.bfloat16)
        mixed = jnp.einsum(
            "kgqs,skd->qkgd",
            softmax_weights,
            v_rows[block_index],
            preferred_element_type=jnp.float32,
        )
        attention_results.append(mixed.astype(jnp.bfloat16).reshape(GROUP_SPAN, kv_heads, width))
    out_sorted = jnp.concatenate(attention_results, axis=0)
    results = out_sorted[jnp.clip(flat_slot, 0, tok_rows - 1)]
    return results.reshape(source_count, slot_count, kv_heads, width)


def shards_by_owner(queries, keys, values, cluster_ids):
    position_numbers = lax.all_gather(cluster_ids, "kv", axis=0, tiled=True)
    tok_rows = position_numbers.shape[0]
    seq_count = lax.axis_size("seq")
    cluster_count = tok_rows // GROUP_SPAN * seq_count
    onehot = (
        position_numbers[:, None] == jnp.arange(cluster_count, dtype=jnp.int32)[None, :]
    ).astype(jnp.int32)
    counts = jnp.sum(onehot, axis=0)
    local_rank = jnp.sum((jnp.cumsum(onehot, axis=0) - onehot) * onehot, axis=1)
    offsets = prefix(
        counts,
        "seq",
        lambda before_part, after_part: before_part + after_part,
        jnp.zeros_like(counts),
    )
    slot_sorted_order = (
        position_numbers * GROUP_SPAN + jnp.sum(onehot * offsets[None, :], axis=1) + local_rank
    ).astype(jnp.int32)
    owner_index = slot_sorted_order // tok_rows
    within = slot_sorted_order % tok_rows
    owner_hot = (owner_index[:, None] == jnp.arange(seq_count, dtype=jnp.int32)[None, :]).astype(
        jnp.int32
    )
    buffer_row = jnp.sum((jnp.cumsum(owner_hot, axis=0) - owner_hot) * owner_hot, axis=1)
    capacity = CLUST_DEV * (GROUP_SPAN // seq_count + max(1, GROUP_SPAN // (2 * seq_count)))
    send_index = owner_index * capacity + buffer_row
    kv_heads = keys.shape[1]
    head_size = keys.shape[2]
    width = queries.shape[1] // kv_heads * head_size
    anchor, filled = source_rows(send_index, seq_count * capacity)
    live = filled[:, None, None]
    q_send = jnp.where(
        live, queries.reshape(tok_rows, kv_heads, width)[anchor], jnp.zeros((), queries.dtype)
    ).reshape(seq_count, capacity, kv_heads, width)
    k_send = jnp.where(live, keys[anchor], jnp.zeros((), keys.dtype)).reshape(
        seq_count, capacity, kv_heads, head_size
    )
    v_send = jnp.where(live, values[anchor], jnp.zeros((), values.dtype)).reshape(
        seq_count, capacity, kv_heads, head_size
    )
    slot_send = jnp.where(filled, within[anchor], -1).reshape(seq_count, capacity)
    query_received, k_recv, v_recv, slot_recv = (
        lax.all_to_all(q_send, "seq", split_axis=0, concat_axis=0, tiled=True),
        lax.all_to_all(k_send, "seq", split_axis=0, concat_axis=0, tiled=True),
        lax.all_to_all(v_send, "seq", split_axis=0, concat_axis=0, tiled=True),
        lax.all_to_all(slot_send, "seq", split_axis=0, concat_axis=0, tiled=True),
    )
    results = attend(query_received, k_recv, v_recv, slot_recv)
    returned = lax.all_to_all(results, "seq", split_axis=0, concat_axis=0, tiled=True)
    mixed = returned.reshape(seq_count * capacity, kv_heads, width)[send_index]
    return mixed.reshape(tok_rows, queries.shape[1], head_size)


CHUNK = 16
TILE = 32
FAR = -1e30
MESH = pl.DeviceIdType.MESH


def ids_kernel(n_seq, n_kv, ids_ref, out_ref, send_sem, recv_sem, own_sem):
    s = lax.axis_index("seq")
    k = lax.axis_index("kv")
    total = n_seq * n_kv
    me = s * n_kv + k
    barrier = pltpu.get_barrier_semaphore()

    def other(i):
        o = lax.rem(me + i, total)
        return {"seq": o // n_kv, "kv": lax.rem(o, n_kv)}

    @pl.loop(1, total)
    def _(i):
        pl.semaphore_signal(barrier, inc=1, device_id=other(i), device_id_type=MESH)

    own = pltpu.make_async_copy(ids_ref, out_ref.at[me], own_sem)
    own.start()
    pl.semaphore_wait(barrier, total - 1)

    def copy(i):
        return pltpu.make_async_remote_copy(
            src_ref=ids_ref,
            dst_ref=out_ref.at[me],
            send_sem=send_sem.at[i],
            recv_sem=recv_sem.at[i],
            device_id=other(i),
            device_id_type=MESH,
        )

    @pl.loop(1, total)
    def _(i):
        copy(i).start()

    @pl.loop(1, total)
    def _(i):
        copy(i).wait()

    own.wait()


def gather_ids(cluster_ids):
    n_seq, n_kv = lax.axis_size("seq"), lax.axis_size("kv")
    total = n_seq * n_kv
    rows = cluster_ids.shape[0] // 128
    return pl.pallas_call(
        functools.partial(ids_kernel, n_seq, n_kv),
        out_shape=jax.ShapeDtypeStruct((total, rows, 128), jnp.int32),
        in_specs=[pl.BlockSpec(memory_space=pltpu.VMEM)],
        out_specs=pl.BlockSpec(memory_space=pltpu.VMEM),
        scratch_shapes=[
            pltpu.SemaphoreType.DMA((total,)),
            pltpu.SemaphoreType.DMA((total,)),
            pltpu.SemaphoreType.DMA,
        ],
        compiler_params=pltpu.CompilerParams(collective_id=0, has_side_effects=True),
        name="gather_ids",
    )(cluster_ids.reshape(rows, 128))


def place(n_z):
    s = lax.axis_index("seq")
    return s // 2, lax.rem(s, 2)


def attend_tile(
    h, group, chunk_count, j, cluster_t, list_t, perm_t, info_t, q_ref, k_ref, v_ref, aug_ref, o_ref,
    qa, kb, vb, ab,
):
    tok_rows, _, width = q_ref.shape
    rows = TILE * group
    near = 256
    factor = math.log2(math.e) / math.sqrt(width)
    c = cluster_t[j]
    base = info_t[0, j]
    rank0 = info_t[1, j]
    shift = info_t[2, j]
    own_cols = info_t[3, j]
    for i in range(TILE):
        token = perm_t[jnp.minimum(base + i, tok_rows - 1)]
        q = q_ref[token].astype(jnp.float32)
        qa[i * group : (i + 1) * group, :] = q[h * group : (h + 1) * group]
    for i in range(chunk_count):
        index = list_t[c * chunk_count + i]
        at = slice(i * CHUNK, (i + 1) * CHUNK)
        ab[at, :] = aug_ref[index]
        kb[at, :] = k_ref[index]
        vb[at, :width] = v_ref[index]
    col = lax.broadcasted_iota(jnp.int32, (rows, near), 1)
    token_row = lax.broadcasted_iota(jnp.int32, (rows, near), 0) // group
    lane = lax.broadcasted_iota(jnp.int32, (rows, 128), 1)
    mark = jnp.where(lane == c, 1.0, 0.0).astype(jnp.bfloat16)
    hidden = (col - token_row > rank0 - shift) & (col < own_cols)
    lhs = jnp.concatenate([qa[...].astype(jnp.bfloat16), mark], axis=1)
    rhs = jnp.concatenate([kb[...], ab[...]], axis=1)
    s = lax.dot_general(lhs, rhs, (((1,), (1,)), ((), ())), preferred_element_type=jnp.float32)
    s = jnp.concatenate([jnp.where(hidden, FAR, s[:, :near]), s[:, near:]], axis=1)
    top = jnp.max(s, axis=1, keepdims=True)
    w = jnp.exp2((s - top) * factor)
    o = jnp.dot(w.astype(jnp.bfloat16), vb[...], preferred_element_type=jnp.float32)
    o = o[:, :width] / o[:, width:]
    o_ref[pl.ds(j * TILE, TILE)] = o.reshape(TILE, group, width)


def rows_kernel(
    n_z, tiles, chunk_count, cluster_t, list_t, perm_t, info_t, low_ref, high_ref, q_hbm, kv_ref,
    later_ref, o_ref, aug_ref,
    first_ref, q_ref, qa, kb, vb, ab, send_sem, recv_sem, extra_send, extra_recv, own_sem, q_sem,
):
    heads = 2
    z, y = place(n_z)
    me = z * 2 + y
    side = z * 2 + 1 - y
    chunks = kv_ref.shape[2]
    barrier = pltpu.get_barrier_semaphore()

    def greet(cond, device):
        @pl.when(cond)
        def _():
            pl.semaphore_signal(barrier, inc=1, device_id={"seq": device}, device_id_type=MESH)

    greet(z >= 0, side)
    greet(z > 0, me - 2)
    greet(z < n_z - 1, me + 2)

    places = (first_ref, later_ref)

    def slot(h, source):
        return places[h].at[:, pl.ds(source * chunks, chunks)]

    own = [pltpu.make_async_copy(kv_ref.at[h], slot(h, me), own_sem.at[h]) for h in range(heads)]
    q_copy = pltpu.make_async_copy(q_hbm, q_ref, q_sem)

    def hop(h, source, src, way):
        return pltpu.make_async_remote_copy(
            src_ref=src,
            dst_ref=slot(h, source),
            send_sem=send_sem.at[h, source, way],
            recv_sem=recv_sem.at[h, source],
            device_id={"seq": me + 2 if way == 0 else side},
            device_id_type=MESH,
        )

    peers = 1 + (z > 0).astype(jnp.int32) + (z < n_z - 1).astype(jnp.int32)
    pl.semaphore_wait(barrier, peers)

    last = z == n_z - 1
    turn = (z == n_z - 2) & (y == 1)

    def half(h, source, part):
        return places[h].at[part, pl.ds(source * chunks, chunks)]

    def first_half(h, source):
        return pltpu.make_async_remote_copy(
            src_ref=half(h, source, 0),
            dst_ref=half(h, source, 0),
            send_sem=send_sem.at[h, source, 1],
            recv_sem=recv_sem.at[h, source],
            device_id={"seq": side},
            device_id_type=MESH,
        )

    def second_half(h, source):
        return pltpu.make_async_remote_copy(
            src_ref=half(h, source, 1),
            dst_ref=half(h, source, 1),
            send_sem=extra_send.at[h],
            recv_sem=extra_recv.at[h],
            device_id={"seq": me + 2},
            device_id_type=MESH,
        )

    def send_own(h):
        @pl.when(z < n_z - 1)
        def _():
            hop(h, me, kv_ref.at[h], 0).start()

        @pl.when(y == 0)
        def _():
            hop(h, me, kv_ref.at[h], 1).start()

    def relay(h, back):
        @pl.when(z >= back)
        def _():
            source = me - 2 * back
            hop(h, source, slot(h, source), 0).wait_recv()

            @pl.when(z < n_z - 1)
            def _():
                hop(h, source, slot(h, source), 0).start()

            if back > 1:
                hop(h, source, slot(h, source), 1).start()
            else:

                @pl.when(last & (y == 0))
                def _():
                    first_half(h, source).start()

                @pl.when(jnp.logical_not(last & (y == 0)))
                def _():
                    hop(h, source, slot(h, source), 1).start()

    def relay_turn(h):
        @pl.when(turn)
        def _():
            hop(h, me - 1, slot(h, me - 1), 1).wait_recv()
            second_half(h, me - 1).start()

    def arrive(h):
        @pl.when((y == 1) & jnp.logical_not(turn))
        def _():
            hop(h, me - 1, slot(h, me - 1), 1).wait_recv()

        for back in range(1, n_z):

            @pl.when(z >= back)
            def _():
                across = side - 2 * back
                if back > 1:
                    hop(h, across, slot(h, across), 1).wait_recv()
                else:

                    @pl.when(last & (y == 1))
                    def _():
                        first_half(h, across).wait_recv()
                        second_half(h, across).wait_recv()

                    @pl.when(jnp.logical_not(last & (y == 1)))
                    def _():
                        hop(h, across, slot(h, across), 1).wait_recv()

    def leave(h):
        @pl.when(turn)
        def _():
            second_half(h, me - 1).wait_send()

        @pl.when(z < n_z - 1)
        def _():
            hop(h, me, kv_ref.at[h], 0).wait_send()

        @pl.when(y == 0)
        def _():
            hop(h, me, kv_ref.at[h], 1).wait_send()

        for back in range(1, n_z):

            @pl.when(z >= back)
            def _():
                source = me - 2 * back

                @pl.when(z < n_z - 1)
                def _():
                    hop(h, source, slot(h, source), 0).wait_send()

                if back > 1:
                    hop(h, source, slot(h, source), 1).wait_send()
                else:

                    @pl.when(last & (y == 0))
                    def _():
                        first_half(h, source).wait_send()

                    @pl.when(jnp.logical_not(last & (y == 0)))
                    def _():
                        hop(h, source, slot(h, source), 1).wait_send()

    send_own(0)
    own[0].start()
    q_copy.start()
    vb[:, q_ref.shape[2] :] = jnp.ones((vb.shape[0], vb.shape[1] - q_ref.shape[2]), jnp.bfloat16)
    row = lax.broadcasted_iota(jnp.int32, (chunks * CHUNK, 128), 0)

    def fill(source, carry):
        within = (row >= low_ref[source]) & (row < high_ref[source])
        aug = jnp.where(within, 0.0, FAR).astype(jnp.bfloat16)
        aug_ref[pl.ds(source * chunks, chunks)] = aug.reshape(chunks, CHUNK, 128)
        return carry

    lax.fori_loop(0, 2 * n_z, fill, 0)
    for back in range(1, n_z):
        relay(0, back)
        if back == 1:
            relay_turn(0)
    send_own(1)
    own[1].start()
    arrive(0)
    own[0].wait()
    q_copy.wait()
    group = o_ref.shape[1]

    def one(j, carry):
        attend_tile(
            0, group, chunk_count, j, cluster_t, list_t, perm_t, info_t, q_ref,
            first_ref.at[0], first_ref.at[1], aug_ref, o_ref, qa, kb, vb, ab,
        )
        return carry

    for back in range(1, n_z + 1):
        lax.fori_loop(tiles * (back - 1) // n_z, tiles * back // n_z, one, 0)
        if back < n_z:
            relay(1, back)
        if back == 1:
            relay_turn(1)
    arrive(1)
    leave(0)
    leave(1)
    own[1].wait()


def gather_rows(kv_own, queries, tables, low, high, tiles, chunk_count):
    n_seq = lax.axis_size("seq")
    heads, two, chunks, chunk, width = kv_own.shape
    group = queries.shape[1] // heads
    span = chunk_count * CHUNK
    hbm = pl.BlockSpec(memory_space=pl.ANY)
    vmem = pl.BlockSpec(memory_space=pltpu.VMEM)
    smem = pl.BlockSpec(memory_space=pltpu.SMEM)
    return pl.pallas_call(
        functools.partial(rows_kernel, n_seq // 2, tiles, chunk_count),
        out_shape=(
            jax.ShapeDtypeStruct((two, n_seq * chunks, chunk, width), kv_own.dtype),
            jax.ShapeDtypeStruct((tiles * TILE, group, width), jnp.float32),
            jax.ShapeDtypeStruct((n_seq * chunks, chunk, 128), jnp.bfloat16),
        ),
        in_specs=[smem] * 4 + [vmem] * 2 + [hbm] * 2,
        out_specs=(hbm, vmem, vmem),
        scratch_shapes=[
            pltpu.VMEM((two, n_seq * chunks, chunk, width), kv_own.dtype),
            pltpu.VMEM(queries.shape, queries.dtype),
            pltpu.VMEM((TILE * group, width), jnp.float32),
            pltpu.VMEM((span, width), jnp.bfloat16),
            pltpu.VMEM((span, 2 * width), jnp.bfloat16),
            pltpu.VMEM((span, 128), jnp.bfloat16),
            pltpu.SemaphoreType.DMA((heads, n_seq, 2)),
            pltpu.SemaphoreType.DMA((heads, n_seq)),
            pltpu.SemaphoreType.DMA((heads,)),
            pltpu.SemaphoreType.DMA((heads,)),
            pltpu.SemaphoreType.DMA((heads,)),
            pltpu.SemaphoreType.DMA,
        ],
        compiler_params=pltpu.CompilerParams(
            collective_id=1, has_side_effects=True, vmem_limit_bytes=48 * 2**20
        ),
        name="gather_rows",
    )(*tables, low, high, queries, kv_own)


def attend_kernel(
    chunk_count, cluster_t, list_t, perm_t, info_t, flat_t,
    q_ref, kv_ref, aug_ref, done_hbm, out_ref, qa, kb, vb, ab, done, obuf, sem,
):
    tok_rows, q_heads, width = q_ref.shape
    group = done.shape[1]
    copy = pltpu.make_async_copy(done_hbm, done, sem)
    copy.start()
    vb[:, width:] = jnp.ones((vb.shape[0], width), jnp.bfloat16)

    def one(j, carry):
        attend_tile(
            1, group, chunk_count, j, cluster_t, list_t, perm_t, info_t, q_ref,
            kv_ref.at[0], kv_ref.at[1], aug_ref, obuf, qa, kb, vb, ab,
        )
        return carry

    lax.fori_loop(0, info_t[4, 0], one, 0)
    copy.wait()

    def put(i, carry):
        for k in range(8):
            t = i * 8 + k
            row = flat_t[t]
            both = jnp.concatenate([done[row], obuf[row]], axis=0)
            out_ref[t] = both.astype(out_ref.dtype)
        return carry

    lax.fori_loop(0, tok_rows // 8, put, 0)


def plan(ids, n_seq):
    i32, bf16, f32 = jnp.int32, jnp.bfloat16, jnp.float32
    tok_rows = ids.shape[1]
    clusters = n_seq * tok_rows // GROUP_SPAN
    chunks = tok_rows // CHUNK
    me = lax.axis_index("seq")
    numbers = jnp.arange(clusters, dtype=i32)
    counts = jnp.sum((ids[:, None, :] == numbers[None, :, None]).astype(i32), axis=2)
    before = (numbers[:, None] < numbers[None, :]).astype(i32)
    start = jnp.sum(counts[:, :, None] * before[None], axis=1)

    ids_me = lax.dynamic_index_in_dim(ids, me, 0, False)
    n_me = lax.dynamic_index_in_dim(counts, me, 0, False)
    start_me = lax.dynamic_index_in_dim(start, me, 0, False)
    where_t = jnp.arange(tok_rows, dtype=i32)
    earlier = (where_t[None, :] < where_t[:, None]) & (ids_me[None, :] == ids_me[:, None])
    rank = jnp.sum(earlier.astype(i32), axis=1)
    hot = (ids_me[:, None] == numbers[None, :]).astype(i32)
    slot = jnp.sum(hot * start_me[None, :], axis=1) + rank
    take = slot[None, :] == where_t[:, None]
    perm = jnp.sum(jnp.where(take, where_t[None, :], 0), axis=1)

    tile_n = (n_me + TILE - 1) // TILE
    tile_start = jnp.sum(tile_n[:, None] * before, axis=0)
    flat = jnp.sum(hot * tile_start[None, :], axis=1) * TILE + rank
    tiles = tok_rows // TILE + clusters
    turn = jnp.arange(tiles, dtype=i32)
    cluster = jnp.sum((tile_start[None, :] + tile_n[None, :] <= turn[:, None]).astype(i32), axis=1)
    cluster = jnp.minimum(cluster, clusters - 1)
    tile_hot = (cluster[:, None] == numbers[None, :]).astype(i32)
    pick = lambda v: jnp.sum(tile_hot * v[None, :], axis=1)
    rank0 = (turn - pick(tile_start)) * TILE
    base = pick(start_me) + rank0

    low = start // CHUNK
    high = (start + counts + CHUNK - 1) // CHUNK
    seen = (jnp.arange(n_seq, dtype=i32) <= me)[:, None] & (counts > 0)
    span = jnp.where(seen, high - low, 0)
    sources = jnp.arange(n_seq, dtype=i32)
    later = (sources[:, None] > sources[None, :]).astype(i32)
    ahead = jnp.sum(span[:, None, :] * later[:, :, None], axis=0)
    chunk_count = (GROUP_SPAN + (2 * CHUNK - 2) * n_seq) // CHUNK
    chunk_count = (chunk_count + 7) // 8 * 8
    at = jnp.arange(chunk_count, dtype=i32)[None, :, None]
    off = at - ahead.T[:, None, :]
    inside = (off >= 0) & (off < span.T[:, None, :])
    index = sources[None, None, :] * chunks + low.T[:, None, :] + off
    none = me * chunks + jnp.where(start_me >= CHUNK, 0, chunks - 1)
    listed = jnp.sum(jnp.where(inside, index, 0), axis=2)
    listed = jnp.where(jnp.any(inside, axis=2), listed, none[:, None])

    low_me = lax.dynamic_index_in_dim(low, me, 0, False)
    span_me = lax.dynamic_index_in_dim(span, me, 0, False)
    info = jnp.stack([base, rank0, pick(low_me * CHUNK - start_me), pick(span_me) * CHUNK, jnp.full_like(base, jnp.sum(tile_n))])

    pad = lambda v: jnp.pad(v, ((0, 0), (0, 128 - clusters)))
    low_row, high_row = pad(start)[:, None, :], pad(start + counts)[:, None, :]
    tables = (cluster, listed.reshape(-1), perm, info)
    return take, tables, flat, low_row, high_row, tiles, chunk_count


def shards_by_rows(queries, keys, values, cluster_ids):
    n_seq = lax.axis_size("seq")
    tok_rows, heads, width = keys.shape
    chunks = tok_rows // CHUNK
    ids = gather_ids(cluster_ids).reshape(n_seq, tok_rows)
    take, tables, flat, low, high, tiles, chunk_count = plan(ids, n_seq)
    pair = jnp.concatenate([keys, values], axis=1).reshape(tok_rows, 2 * heads * width)
    moved = jnp.dot(take.astype(jnp.bfloat16), pair, preferred_element_type=jnp.float32)
    moved = moved.astype(jnp.bfloat16).reshape(chunks, CHUNK, 2, heads, width)
    kv_own = jnp.transpose(moved, (3, 2, 0, 1, 4))
    kv, done, aug = gather_rows(kv_own, queries, tables, low, high, tiles, chunk_count)
    group = queries.shape[1] // heads
    span = chunk_count * CHUNK
    vmem = pl.BlockSpec(memory_space=pltpu.VMEM)
    smem = pl.BlockSpec(memory_space=pltpu.SMEM)
    return pl.pallas_call(
        functools.partial(attend_kernel, chunk_count),
        out_shape=jax.ShapeDtypeStruct(queries.shape, queries.dtype),
        in_specs=[smem] * 5 + [vmem] * 3 + [pl.BlockSpec(memory_space=pl.ANY)],
        out_specs=vmem,
        scratch_shapes=[
            pltpu.VMEM((TILE * group, width), jnp.float32),
            pltpu.VMEM((span, width), jnp.bfloat16),
            pltpu.VMEM((span, 2 * width), jnp.bfloat16),
            pltpu.VMEM((span, 128), jnp.bfloat16),
            pltpu.VMEM(done.shape, jnp.float32),
            pltpu.VMEM(done.shape, jnp.float32),
            pltpu.SemaphoreType.DMA,
        ],
        compiler_params=pltpu.CompilerParams(vmem_limit_bytes=48 * 2**20),
        name="attend_rows",
    )(*tables, flat, queries, kv, aug, done)


def solution(mesh):
    in_specs = (P("seq", "kv", None), P("seq", "kv", None), P("seq", "kv", None), P(("seq", "kv")))
    out_specs = P("seq", "kv", None)
    fits = 4 <= mesh.shape["seq"] <= 8 and mesh.shape["seq"] % 2 == 0
    body = shards_by_rows if fits else shards_by_owner
    return jax.shard_map(body, mesh=mesh, in_specs=in_specs, out_specs=out_specs, check_vma=False)
```

```python
import functools
import math

import jax
import jax.numpy as jnp
from jax import lax
from jax.experimental import pallas as pl
from jax.experimental.pallas import tpu as pltpu
from jax.sharding import PartitionSpec as P

GROUP_SPAN = 512
CLUST_DEV = 2


def prefix(part, axis, combine, identity):
    place = lax.axis_index(axis)
    gathered = lax.all_gather(part, axis)
    state = jnp.zeros_like(part) + jnp.asarray(identity, part.dtype)

    def one(turn, state):
        return combine(state, lax.dynamic_index_in_dim(gathered, turn, 0, False))

    return lax.fori_loop(0, place, one, state)


def source_rows(target_index, slot_total):
    source_total = target_index.shape[0]
    hits = target_index[None, :] == jnp.arange(slot_total, dtype=jnp.int32)[:, None]
    numbers = jnp.arange(source_total, dtype=jnp.int32)[None, :]
    anchor = jnp.sum(jnp.where(hits, numbers, 0), axis=1)
    filled = jnp.any(hits, axis=1)
    return (anchor, filled)


def attend(query_received, k_recv, v_recv, row_slot):
    source_count, slot_count, kv_heads, width = query_received.shape
    head_size = k_recv.shape[3]
    group_size = width // head_size
    tok_rows = CLUST_DEV * GROUP_SPAN
    flat_slot = row_slot.reshape(source_count * slot_count)
    anchor, filled = source_rows(flat_slot, tok_rows)
    q_flat = query_received.reshape(source_count * slot_count, kv_heads, width)
    k_flat = k_recv.reshape(source_count * slot_count, kv_heads, head_size)
    v_flat = v_recv.reshape(source_count * slot_count, kv_heads, head_size)
    live = filled[:, None, None]
    q_rows = jnp.where(live, q_flat[anchor], jnp.zeros((), q_flat.dtype))
    k_rows = jnp.where(live, k_flat[anchor], jnp.zeros((), k_flat.dtype))
    v_rows = jnp.where(live, v_flat[anchor], jnp.zeros((), v_flat.dtype))
    q_rows = q_rows.reshape(CLUST_DEV, GROUP_SPAN, kv_heads, group_size, head_size)
    k_rows = k_rows.reshape(CLUST_DEV, GROUP_SPAN, kv_heads, head_size)
    v_rows = v_rows.reshape(CLUST_DEV, GROUP_SPAN, kv_heads, head_size)
    causal = jnp.arange(GROUP_SPAN)[:, None] >= jnp.arange(GROUP_SPAN)[None, :]
    score_scale = 1.0 / math.sqrt(head_size)
    attention_results = []
    for block_index in range(CLUST_DEV):
        scores = (
            jnp.einsum(
                "qkgd,skd->kgqs",
                q_rows[block_index],
                k_rows[block_index],
                preferred_element_type=jnp.float32,
            )
            * score_scale
        )
        scores = jnp.where(causal, scores, -jnp.inf)
        row_max = jnp.max(scores, axis=-1, keepdims=True)
        weights = jnp.exp(scores - row_max)
        softmax_weights = (weights / jnp.sum(weights, axis=-1, keepdims=True)).astype(jnp.bfloat16)
        mixed = jnp.einsum(
            "kgqs,skd->qkgd",
            softmax_weights,
            v_rows[block_index],
            preferred_element_type=jnp.float32,
        )
        attention_results.append(mixed.astype(jnp.bfloat16).reshape(GROUP_SPAN, kv_heads, width))
    out_sorted = jnp.concatenate(attention_results, axis=0)
    results = out_sorted[jnp.clip(flat_slot, 0, tok_rows - 1)]
    return results.reshape(source_count, slot_count, kv_heads, width)


def shards_by_owner(queries, keys, values, cluster_ids):
    position_numbers = lax.all_gather(cluster_ids, "kv", axis=0, tiled=True)
    tok_rows = position_numbers.shape[0]
    seq_count = lax.axis_size("seq")
    cluster_count = tok_rows // GROUP_SPAN * seq_count
    onehot = (
        position_numbers[:, None] == jnp.arange(cluster_count, dtype=jnp.int32)[None, :]
    ).astype(jnp.int32)
    counts = jnp.sum(onehot, axis=0)
    local_rank = jnp.sum((jnp.cumsum(onehot, axis=0) - onehot) * onehot, axis=1)
    offsets = prefix(
        counts,
        "seq",
        lambda before_part, after_part: before_part + after_part,
        jnp.zeros_like(counts),
    )
    slot_sorted_order = (
        position_numbers * GROUP_SPAN + jnp.sum(onehot * offsets[None, :], axis=1) + local_rank
    ).astype(jnp.int32)
    owner_index = slot_sorted_order // tok_rows
    within = slot_sorted_order % tok_rows
    owner_hot = (owner_index[:, None] == jnp.arange(seq_count, dtype=jnp.int32)[None, :]).astype(
        jnp.int32
    )
    buffer_row = jnp.sum((jnp.cumsum(owner_hot, axis=0) - owner_hot) * owner_hot, axis=1)
    capacity = CLUST_DEV * (GROUP_SPAN // seq_count + max(1, GROUP_SPAN // (2 * seq_count)))
    send_index = owner_index * capacity + buffer_row
    kv_heads = keys.shape[1]
    head_size = keys.shape[2]
    width = queries.shape[1] // kv_heads * head_size
    anchor, filled = source_rows(send_index, seq_count * capacity)
    live = filled[:, None, None]
    q_send = jnp.where(
        live, queries.reshape(tok_rows, kv_heads, width)[anchor], jnp.zeros((), queries.dtype)
    ).reshape(seq_count, capacity, kv_heads, width)
    k_send = jnp.where(live, keys[anchor], jnp.zeros((), keys.dtype)).reshape(
        seq_count, capacity, kv_heads, head_size
    )
    v_send = jnp.where(live, values[anchor], jnp.zeros((), values.dtype)).reshape(
        seq_count, capacity, kv_heads, head_size
    )
    slot_send = jnp.where(filled, within[anchor], -1).reshape(seq_count, capacity)
    query_received, k_recv, v_recv, slot_recv = (
        lax.all_to_all(q_send, "seq", split_axis=0, concat_axis=0, tiled=True),
        lax.all_to_all(k_send, "seq", split_axis=0, concat_axis=0, tiled=True),
        lax.all_to_all(v_send, "seq", split_axis=0, concat_axis=0, tiled=True),
        lax.all_to_all(slot_send, "seq", split_axis=0, concat_axis=0, tiled=True),
    )
    results = attend(query_received, k_recv, v_recv, slot_recv)
    returned = lax.all_to_all(results, "seq", split_axis=0, concat_axis=0, tiled=True)
    mixed = returned.reshape(seq_count * capacity, kv_heads, width)[send_index]
    return mixed.reshape(tok_rows, queries.shape[1], head_size)


CHUNK = 16
TILE = 32
FAR = -1e30
MESH = pl.DeviceIdType.MESH


def ids_kernel(n_seq, n_kv, ids_ref, out_ref, send_sem, recv_sem, own_sem):
    s = lax.axis_index("seq")
    k = lax.axis_index("kv")
    total = n_seq * n_kv
    me = s * n_kv + k
    barrier = pltpu.get_barrier_semaphore()

    def other(i):
        o = lax.rem(me + i, total)
        return {"seq": o // n_kv, "kv": lax.rem(o, n_kv)}

    @pl.loop(1, total)
    def _(i):
        pl.semaphore_signal(barrier, inc=1, device_id=other(i), device_id_type=MESH)

    own = pltpu.make_async_copy(ids_ref, out_ref.at[me], own_sem)
    own.start()
    pl.semaphore_wait(barrier, total - 1)

    def copy(i):
        return pltpu.make_async_remote_copy(
            src_ref=ids_ref,
            dst_ref=out_ref.at[me],
            send_sem=send_sem.at[i],
            recv_sem=recv_sem.at[i],
            device_id=other(i),
            device_id_type=MESH,
        )

    @pl.loop(1, total)
    def _(i):
        copy(i).start()

    @pl.loop(1, total)
    def _(i):
        copy(i).wait()

    own.wait()


def gather_ids(cluster_ids):
    n_seq, n_kv = lax.axis_size("seq"), lax.axis_size("kv")
    total = n_seq * n_kv
    rows = cluster_ids.shape[0] // 128
    return pl.pallas_call(
        functools.partial(ids_kernel, n_seq, n_kv),
        out_shape=jax.ShapeDtypeStruct((total, rows, 128), jnp.int32),
        in_specs=[pl.BlockSpec(memory_space=pltpu.VMEM)],
        out_specs=pl.BlockSpec(memory_space=pltpu.VMEM),
        scratch_shapes=[
            pltpu.SemaphoreType.DMA((total,)),
            pltpu.SemaphoreType.DMA((total,)),
            pltpu.SemaphoreType.DMA,
        ],
        compiler_params=pltpu.CompilerParams(collective_id=0, has_side_effects=True),
        name="gather_ids",
    )(cluster_ids.reshape(rows, 128))


def place(n_z):
    s = lax.axis_index("seq")
    return s // 2, lax.rem(s, 2)


def collect_tile(
    k, h, group, chunk_count, j, cluster_t, list_t, perm_t, info_t, q_ref, k_ref, v_ref, aug_ref,
    qa, kb, vb, ab,
):
    tok_rows, _, width = q_ref.shape
    c = cluster_t[j]
    base = info_t[0, j]
    for i in range(TILE):
        token = perm_t[jnp.minimum(base + i, tok_rows - 1)]
        q = q_ref[token].astype(jnp.float32)
        qa[k, i * group : (i + 1) * group, :] = q[h * group : (h + 1) * group]
    for i in range(chunk_count):
        index = list_t[c * chunk_count + i]
        at = slice(i * CHUNK, (i + 1) * CHUNK)
        ab[k, at, :] = aug_ref[index]
        kb[k, at, :] = k_ref[index]
        vb[k, at, :width] = v_ref[index]


def attend_tile(k, group, j, cluster_t, info_t, o_ref, qa, kb, vb, ab):
    _, rows, width = qa.shape
    near = 256
    factor = math.log2(math.e) / math.sqrt(width)
    c = cluster_t[j]
    rank0 = info_t[1, j]
    shift = info_t[2, j]
    own_cols = info_t[3, j]
    col = lax.broadcasted_iota(jnp.int32, (rows, near), 1)
    token_row = lax.broadcasted_iota(jnp.int32, (rows, near), 0) // group
    lane = lax.broadcasted_iota(jnp.int32, (rows, 128), 1)
    mark = jnp.where(lane == c, 1.0, 0.0).astype(jnp.bfloat16)
    hidden = (col - token_row > rank0 - shift) & (col < own_cols)
    lhs = jnp.concatenate([qa[k].astype(jnp.bfloat16), mark], axis=1)
    rhs = jnp.concatenate([kb[k], ab[k]], axis=1)
    s = lax.dot_general(lhs, rhs, (((1,), (1,)), ((), ())), preferred_element_type=jnp.float32)
    s = jnp.concatenate([jnp.where(hidden, FAR, s[:, :near]), s[:, near:]], axis=1)
    top = jnp.max(s, axis=1, keepdims=True)
    w = jnp.exp2((s - top) * factor)
    o = jnp.dot(w.astype(jnp.bfloat16), vb[k], preferred_element_type=jnp.float32)
    o = o[:, :width] / o[:, width:]
    o_ref[pl.ds(j * TILE, TILE)] = o.reshape(TILE, group, width)


def rows_kernel(
    n_z, tiles, chunk_count, cluster_t, list_t, perm_t, info_t, low_ref, high_ref, q_hbm, kv_ref,
    later_ref, o_ref, aug_ref,
    first_ref, q_ref, qa, kb, vb, ab, send_sem, recv_sem, extra_send, extra_recv, own_sem, q_sem,
):
    heads = 2
    z, y = place(n_z)
    me = z * 2 + y
    side = z * 2 + 1 - y
    chunks = kv_ref.shape[2]
    barrier = pltpu.get_barrier_semaphore()

    def greet(cond, device):
        @pl.when(cond)
        def _():
            pl.semaphore_signal(barrier, inc=1, device_id={"seq": device}, device_id_type=MESH)

    greet(z >= 0, side)
    greet(z > 0, me - 2)
    greet(z < n_z - 1, me + 2)

    places = (first_ref, later_ref)

    def slot(h, source):
        return places[h].at[:, pl.ds(source * chunks, chunks)]

    own = [pltpu.make_async_copy(kv_ref.at[h], slot(h, me), own_sem.at[h]) for h in range(heads)]
    q_copy = pltpu.make_async_copy(q_hbm, q_ref, q_sem)

    def hop(h, source, src, way):
        return pltpu.make_async_remote_copy(
            src_ref=src,
            dst_ref=slot(h, source),
            send_sem=send_sem.at[h, source, way],
            recv_sem=recv_sem.at[h, source],
            device_id={"seq": me + 2 if way == 0 else side},
            device_id_type=MESH,
        )

    peers = 1 + (z > 0).astype(jnp.int32) + (z < n_z - 1).astype(jnp.int32)
    pl.semaphore_wait(barrier, peers)

    last = z == n_z - 1
    turn = (z == n_z - 2) & (y == 1)

    def half(h, source, part):
        return places[h].at[part, pl.ds(source * chunks, chunks)]

    def first_half(h, source):
        return pltpu.make_async_remote_copy(
            src_ref=half(h, source, 0),
            dst_ref=half(h, source, 0),
            send_sem=send_sem.at[h, source, 1],
            recv_sem=recv_sem.at[h, source],
            device_id={"seq": side},
            device_id_type=MESH,
        )

    def second_half(h, source):
        return pltpu.make_async_remote_copy(
            src_ref=half(h, source, 1),
            dst_ref=half(h, source, 1),
            send_sem=extra_send.at[h],
            recv_sem=extra_recv.at[h],
            device_id={"seq": me + 2},
            device_id_type=MESH,
        )

    def send_own(h):
        @pl.when(z < n_z - 1)
        def _():
            hop(h, me, kv_ref.at[h], 0).start()

        @pl.when(y == 0)
        def _():
            hop(h, me, kv_ref.at[h], 1).start()

    def relay(h, back):
        @pl.when(z >= back)
        def _():
            source = me - 2 * back
            hop(h, source, slot(h, source), 0).wait_recv()

            @pl.when(z < n_z - 1)
            def _():
                hop(h, source, slot(h, source), 0).start()

            if back > 1:
                hop(h, source, slot(h, source), 1).start()
            else:

                @pl.when(last & (y == 0))
                def _():
                    first_half(h, source).start()

                @pl.when(jnp.logical_not(last & (y == 0)))
                def _():
                    hop(h, source, slot(h, source), 1).start()

    def relay_turn(h):
        @pl.when(turn)
        def _():
            hop(h, me - 1, slot(h, me - 1), 1).wait_recv()
            second_half(h, me - 1).start()

    def arrive(h):
        @pl.when((y == 1) & jnp.logical_not(turn))
        def _():
            hop(h, me - 1, slot(h, me - 1), 1).wait_recv()

        for back in range(1, n_z):

            @pl.when(z >= back)
            def _():
                across = side - 2 * back
                if back > 1:
                    hop(h, across, slot(h, across), 1).wait_recv()
                else:

                    @pl.when(last & (y == 1))
                    def _():
                        first_half(h, across).wait_recv()
                        second_half(h, across).wait_recv()

                    @pl.when(jnp.logical_not(last & (y == 1)))
                    def _():
                        hop(h, across, slot(h, across), 1).wait_recv()

    def leave(h):
        @pl.when(turn)
        def _():
            second_half(h, me - 1).wait_send()

        @pl.when(z < n_z - 1)
        def _():
            hop(h, me, kv_ref.at[h], 0).wait_send()

        @pl.when(y == 0)
        def _():
            hop(h, me, kv_ref.at[h], 1).wait_send()

        for back in range(1, n_z):

            @pl.when(z >= back)
            def _():
                source = me - 2 * back

                @pl.when(z < n_z - 1)
                def _():
                    hop(h, source, slot(h, source), 0).wait_send()

                if back > 1:
                    hop(h, source, slot(h, source), 1).wait_send()
                else:

                    @pl.when(last & (y == 0))
                    def _():
                        first_half(h, source).wait_send()

                    @pl.when(jnp.logical_not(last & (y == 0)))
                    def _():
                        hop(h, source, slot(h, source), 1).wait_send()

    send_own(0)
    own[0].start()
    q_copy.start()
    ones = (2, vb.shape[1], vb.shape[2] - q_ref.shape[2])
    vb[:, :, q_ref.shape[2] :] = jnp.ones(ones, jnp.bfloat16)
    row = lax.broadcasted_iota(jnp.int32, (chunks * CHUNK, 128), 0)

    def fill(source, carry):
        within = (row >= low_ref[source]) & (row < high_ref[source])
        aug = jnp.where(within, 0.0, FAR).astype(jnp.bfloat16)
        aug_ref[pl.ds(source * chunks, chunks)] = aug.reshape(chunks, CHUNK, 128)
        return carry

    lax.fori_loop(0, 2 * n_z, fill, 0)
    for back in range(1, n_z):
        relay(0, back)
        if back == 1:
            relay_turn(0)
    send_own(1)
    own[1].start()
    arrive(0)
    own[0].wait()
    q_copy.wait()
    group = o_ref.shape[1]

    def one(j, carry):
        for k in range(2):
            collect_tile(
                k, 0, group, chunk_count, 2 * j + k, cluster_t, list_t, perm_t, info_t, q_ref,
                first_ref.at[0], first_ref.at[1], aug_ref, qa, kb, vb, ab,
            )
        for k in range(2):
            attend_tile(k, group, 2 * j + k, cluster_t, info_t, o_ref, qa, kb, vb, ab)
        return carry

    pairs = tiles // 2
    for back in range(1, n_z + 1):
        lax.fori_loop(pairs * (back - 1) // n_z, pairs * back // n_z, one, 0)
        if back < n_z:
            relay(1, back)
        if back == 1:
            relay_turn(1)
    arrive(1)
    leave(0)
    leave(1)
    own[1].wait()


def gather_rows(kv_own, queries, tables, low, high, tiles, chunk_count):
    n_seq = lax.axis_size("seq")
    heads, two, chunks, chunk, width = kv_own.shape
    group = queries.shape[1] // heads
    span = chunk_count * CHUNK
    hbm = pl.BlockSpec(memory_space=pl.ANY)
    vmem = pl.BlockSpec(memory_space=pltpu.VMEM)
    smem = pl.BlockSpec(memory_space=pltpu.SMEM)
    return pl.pallas_call(
        functools.partial(rows_kernel, n_seq // 2, tiles, chunk_count),
        out_shape=(
            jax.ShapeDtypeStruct((two, n_seq * chunks, chunk, width), kv_own.dtype),
            jax.ShapeDtypeStruct((tiles * TILE, group, width), jnp.float32),
            jax.ShapeDtypeStruct((n_seq * chunks, chunk, 128), jnp.bfloat16),
        ),
        in_specs=[smem] * 4 + [vmem] * 2 + [hbm] * 2,
        out_specs=(hbm, vmem, vmem),
        scratch_shapes=[
            pltpu.VMEM((two, n_seq * chunks, chunk, width), kv_own.dtype),
            pltpu.VMEM(queries.shape, queries.dtype),
            pltpu.VMEM((2, TILE * group, width), jnp.float32),
            pltpu.VMEM((2, span, width), jnp.bfloat16),
            pltpu.VMEM((2, span, 2 * width), jnp.bfloat16),
            pltpu.VMEM((2, span, 128), jnp.bfloat16),
            pltpu.SemaphoreType.DMA((heads, n_seq, 2)),
            pltpu.SemaphoreType.DMA((heads, n_seq)),
            pltpu.SemaphoreType.DMA((heads,)),
            pltpu.SemaphoreType.DMA((heads,)),
            pltpu.SemaphoreType.DMA((heads,)),
            pltpu.SemaphoreType.DMA,
        ],
        compiler_params=pltpu.CompilerParams(
            collective_id=1, has_side_effects=True, vmem_limit_bytes=48 * 2**20
        ),
        name="gather_rows",
    )(*tables, low, high, queries, kv_own)


def attend_kernel(
    chunk_count, cluster_t, list_t, perm_t, info_t, flat_t,
    q_ref, kv_ref, aug_ref, done_hbm, out_ref, qa, kb, vb, ab, done, obuf, sem,
):
    tok_rows, q_heads, width = q_ref.shape
    group = done.shape[1]
    copy = pltpu.make_async_copy(done_hbm, done, sem)
    copy.start()
    vb[:, :, width:] = jnp.ones((2, vb.shape[1], width), jnp.bfloat16)

    def one(j, carry):
        for k in range(2):
            collect_tile(
                k, 1, group, chunk_count, 2 * j + k, cluster_t, list_t, perm_t, info_t, q_ref,
                kv_ref.at[0], kv_ref.at[1], aug_ref, qa, kb, vb, ab,
            )
        for k in range(2):
            attend_tile(k, group, 2 * j + k, cluster_t, info_t, obuf, qa, kb, vb, ab)
        return carry

    lax.fori_loop(0, (info_t[4, 0] + 1) // 2, one, 0)
    copy.wait()

    def put(i, carry):
        for k in range(8):
            t = i * 8 + k
            row = flat_t[t]
            both = jnp.concatenate([done[row], obuf[row]], axis=0)
            out_ref[t] = both.astype(out_ref.dtype)
        return carry

    lax.fori_loop(0, tok_rows // 8, put, 0)


def plan(ids, n_seq):
    i32, bf16, f32 = jnp.int32, jnp.bfloat16, jnp.float32
    tok_rows = ids.shape[1]
    clusters = n_seq * tok_rows // GROUP_SPAN
    chunks = tok_rows // CHUNK
    me = lax.axis_index("seq")
    numbers = jnp.arange(clusters, dtype=i32)
    counts = jnp.sum((ids[:, None, :] == numbers[None, :, None]).astype(i32), axis=2)
    before = (numbers[:, None] < numbers[None, :]).astype(i32)
    start = jnp.sum(counts[:, :, None] * before[None], axis=1)

    ids_me = lax.dynamic_index_in_dim(ids, me, 0, False)
    n_me = lax.dynamic_index_in_dim(counts, me, 0, False)
    start_me = lax.dynamic_index_in_dim(start, me, 0, False)
    where_t = jnp.arange(tok_rows, dtype=i32)
    earlier = (where_t[None, :] < where_t[:, None]) & (ids_me[None, :] == ids_me[:, None])
    rank = jnp.sum(earlier.astype(i32), axis=1)
    hot = (ids_me[:, None] == numbers[None, :]).astype(i32)
    slot = jnp.sum(hot * start_me[None, :], axis=1) + rank
    take = slot[None, :] == where_t[:, None]
    perm = jnp.sum(jnp.where(take, where_t[None, :], 0), axis=1)

    tile_n = (n_me + TILE - 1) // TILE
    tile_start = jnp.sum(tile_n[:, None] * before, axis=0)
    flat = jnp.sum(hot * tile_start[None, :], axis=1) * TILE + rank
    tiles = (tok_rows // TILE + clusters + 1) // 2 * 2
    turn = jnp.arange(tiles, dtype=i32)
    cluster = jnp.sum((tile_start[None, :] + tile_n[None, :] <= turn[:, None]).astype(i32), axis=1)
    cluster = jnp.minimum(cluster, clusters - 1)
    tile_hot = (cluster[:, None] == numbers[None, :]).astype(i32)
    pick = lambda v: jnp.sum(tile_hot * v[None, :], axis=1)
    rank0 = (turn - pick(tile_start)) * TILE
    base = pick(start_me) + rank0

    low = start // CHUNK
    high = (start + counts + CHUNK - 1) // CHUNK
    seen = (jnp.arange(n_seq, dtype=i32) <= me)[:, None] & (counts > 0)
    span = jnp.where(seen, high - low, 0)
    sources = jnp.arange(n_seq, dtype=i32)
    later = (sources[:, None] > sources[None, :]).astype(i32)
    ahead = jnp.sum(span[:, None, :] * later[:, :, None], axis=0)
    chunk_count = (GROUP_SPAN + (2 * CHUNK - 2) * n_seq) // CHUNK
    chunk_count = (chunk_count + 7) // 8 * 8
    at = jnp.arange(chunk_count, dtype=i32)[None, :, None]
    off = at - ahead.T[:, None, :]
    inside = (off >= 0) & (off < span.T[:, None, :])
    index = sources[None, None, :] * chunks + low.T[:, None, :] + off
    none = me * chunks + jnp.where(start_me >= CHUNK, 0, chunks - 1)
    listed = jnp.sum(jnp.where(inside, index, 0), axis=2)
    listed = jnp.where(jnp.any(inside, axis=2), listed, none[:, None])

    low_me = lax.dynamic_index_in_dim(low, me, 0, False)
    span_me = lax.dynamic_index_in_dim(span, me, 0, False)
    info = jnp.stack([base, rank0, pick(low_me * CHUNK - start_me), pick(span_me) * CHUNK, jnp.full_like(base, jnp.sum(tile_n))])

    pad = lambda v: jnp.pad(v, ((0, 0), (0, 128 - clusters)))
    low_row, high_row = pad(start)[:, None, :], pad(start + counts)[:, None, :]
    tables = (cluster, listed.reshape(-1), perm, info)
    return take, tables, flat, low_row, high_row, tiles, chunk_count


def shards_by_rows(queries, keys, values, cluster_ids):
    n_seq = lax.axis_size("seq")
    tok_rows, heads, width = keys.shape
    chunks = tok_rows // CHUNK
    ids = gather_ids(cluster_ids).reshape(n_seq, tok_rows)
    take, tables, flat, low, high, tiles, chunk_count = plan(ids, n_seq)
    pair = jnp.concatenate([keys, values], axis=1).reshape(tok_rows, 2 * heads * width)
    moved = jnp.dot(take.astype(jnp.bfloat16), pair, preferred_element_type=jnp.float32)
    moved = moved.astype(jnp.bfloat16).reshape(chunks, CHUNK, 2, heads, width)
    kv_own = jnp.transpose(moved, (3, 2, 0, 1, 4))
    kv, done, aug = gather_rows(kv_own, queries, tables, low, high, tiles, chunk_count)
    group = queries.shape[1] // heads
    span = chunk_count * CHUNK
    vmem = pl.BlockSpec(memory_space=pltpu.VMEM)
    smem = pl.BlockSpec(memory_space=pltpu.SMEM)
    return pl.pallas_call(
        functools.partial(attend_kernel, chunk_count),
        out_shape=jax.ShapeDtypeStruct(queries.shape, queries.dtype),
        in_specs=[smem] * 5 + [vmem] * 3 + [pl.BlockSpec(memory_space=pl.ANY)],
        out_specs=vmem,
        scratch_shapes=[
            pltpu.VMEM((2, TILE * group, width), jnp.float32),
            pltpu.VMEM((2, span, width), jnp.bfloat16),
            pltpu.VMEM((2, span, 2 * width), jnp.bfloat16),
            pltpu.VMEM((2, span, 128), jnp.bfloat16),
            pltpu.VMEM(done.shape, jnp.float32),
            pltpu.VMEM(done.shape, jnp.float32),
            pltpu.SemaphoreType.DMA,
        ],
        compiler_params=pltpu.CompilerParams(vmem_limit_bytes=48 * 2**20),
        name="attend_rows",
    )(*tables, flat, queries, kv, aug, done)


def solution(mesh):
    in_specs = (P("seq", "kv", None), P("seq", "kv", None), P("seq", "kv", None), P(("seq", "kv")))
    out_specs = P("seq", "kv", None)
    fits = 4 <= mesh.shape["seq"] <= 8 and mesh.shape["seq"] % 2 == 0
    body = shards_by_rows if fits else shards_by_owner
    return jax.shard_map(body, mesh=mesh, in_specs=in_specs, out_specs=out_specs, check_vma=False)
```
